32 devices in a mesh: tok: 4 (over y, x), mem: 4 (over z), row: 2 (over core).
Axes of the slice: x: 2, y: 2, z: 4, core: 2. Of those that a mesh axis runs over, the one named last changes fastest.
Arguments:
- queries: bfloat16 [2, 2048, 8192], P(None, ('tok', 'row'), 'mem'), may hold values from -55 to 55
- keys: bfloat16 [2, 2048, 8192], P(None, ('tok', 'row'), 'mem'), may hold values from -3 to 3
- values: bfloat16 [2, 2048, 8192], P(None, ('tok', 'row'), 'mem'), may hold values from -6 to 6
- token_lr: float32 [16, 2, 2048], P('mem', None, ('tok', 'row')), may hold values from 0.05 to 0.5
- momentum_rate: float32 [16], P('mem'), may hold values from 0.3 to 0.9
- update_step: float32 [16], P('mem'), may hold values from 0.2 to 0.6
- fast_weights: float32 [16, 3, 512, 512], P('mem', None, 'row'), may hold values from -0.25 to 0.25
- momentum: float32 [16, 3, 512, 512], P('mem', None, 'row'), may hold values from -24 to 24
Outputs:
- mixed: bfloat16 [2, 2048, 8192], P(None, ('tok', 'row'), 'mem')
- new_weights: float32 [16, 3, 512, 512], P('mem', None, 'row')
- new_momentum: float32 [16, 3, 512, 512], P('mem', None, 'row')
The draws below stay inside these ranges and needn't reach their ends.
All inputs are finite; a program needn't handle non-finite values.
Results may differ from the reference program's by a relative error of at most 0.02.
Values may be sent and summed in bfloat16 or wider, within the bound.
No kernel may reach another device: no remote copies, remote signals or barrier semaphores. Data moves between devices by JAX's collectives and lax.ppermute only.
A program may use at most 192 MiB of HBM per device.

```python
import math
import jax
import jax.numpy as jnp
from jax import lax

HEADS = 16
DH = 512
D = 8192
HEAD_DIM = 128
ATTN_HEADS = 64
WINDOW = 256
NS_STEPS = 2
GROUPS = 2
GROUP = 2048


def draw_pair(key):
    base = jax.random.fold_in(key, 31)
    key_a, key_b = jax.random.split(base, 2)
    total = GROUPS * GROUP
    shape = (total, D)
    queries = jnp.clip(jax.random.normal(key_a, shape, jnp.float32), -3.0, 3.0)
    keys = jnp.clip(jax.random.normal(key_b, shape, jnp.float32), -3.0, 3.0)
    return (queries.reshape(GROUPS, GROUP, D), keys.reshape(GROUPS, GROUP, D))


def draw_queries(key, part):
    return draw_pair(key)[0].astype(jnp.bfloat16)


def draw_keys(key, part):
    return draw_pair(key)[1].astype(jnp.bfloat16)


def block_scale(rng, dims, shards, low, high):
    loudness = 1.0
    for dim, blocks in shards:
        draws = jax.random.uniform(jax.random.fold_in(jax.random.fold_in(rng, 6), dim), (blocks,), jnp.float32, low / len(shards), high / len(shards))
        loudness = loudness * jnp.repeat(jnp.exp(draws), dims[dim] // blocks).reshape((-1,) + (1,) * (len(dims) - 1 - dim))
    return loudness


def noise(own_key, dims, width, most, cuts=(), kind=jnp.bfloat16):
    gain = block_scale(own_key, dims, cuts, -0.22, 0.18) if cuts else 1.0
    values = jax.random.normal(own_key, dims, jnp.float32) * width * gain
    return jnp.minimum(jnp.maximum(values, -most), most).astype(kind)


def setup_inputs(seed: int = 0) -> dict:
    arg_keys = jax.random.split(jax.random.key(seed), 9)
    return {
        "queries": draw_queries(jax.random.fold_in(arg_keys[8], 71), 0),
        "keys": draw_keys(jax.random.fold_in(arg_keys[8], 71), 0),
        "values": noise(arg_keys[2], (GROUPS, GROUP, D), 1.0, 6.0, ((1, 8), (2, 4))),
        "token_lr": jnp.clip(jnp.exp(math.log(0.5) - 2.3025851 * jax.random.uniform(arg_keys[3], (HEADS, GROUPS, GROUP), jnp.float32) ** block_scale(arg_keys[3], (HEADS, GROUPS, GROUP), ((0, 4), (2, 8)), -0.2, 0.2)), 0.05, 0.5),
        "momentum_rate": jnp.clip(0.3 + 0.59999996 * jax.random.uniform(arg_keys[4], (HEADS,), jnp.float32) ** block_scale(arg_keys[4], (HEADS,), ((0, 4),), -0.2, 0.2), 0.3, 0.9),
        "update_step": jnp.clip(0.2 + 0.400000021 * jax.random.uniform(arg_keys[5], (HEADS,), jnp.float32) ** block_scale(arg_keys[5], (HEADS,), ((0, 4),), -0.2, 0.2), 0.2, 0.6),
        "fast_weights": noise(arg_keys[6], (HEADS, 3, DH, DH), DH ** -0.5, 0.25, ((0, 4), (2, 2)), jnp.float32),
        "momentum": noise(arg_keys[7], (HEADS, 3, DH, DH), 4.0, 24.0, ((0, 4), (2, 2)), jnp.float32),
    }


quintic_one = 3.4445
quintic_two = -4.775
quintic_three = 2.0315

def unit_rows(field):
    field = field.astype(jnp.float32)
    return field * lax.rsqrt(lax.optimization_barrier(jnp.mean(field * field, axis=-1, keepdims=True)) + 1e-05)

def refine(ortho, gram):
    gram_half = gram.astype(jnp.bfloat16).astype(jnp.float32)
    square = jnp.einsum('hmde,hmef->hmdf', gram_half, gram_half)
    poly = (quintic_two * gram + quintic_three * square).astype(jnp.bfloat16).astype(jnp.float32)
    turned = jnp.einsum('hmrd,hmde->hmre', ortho.astype(jnp.float32), poly)
    return (quintic_one * ortho.astype(jnp.float32) + turned).astype(jnp.bfloat16)

def attention(queries, keys, values):
    total = GROUPS * GROUP
    seq_queries = queries.reshape(total, ATTN_HEADS, HEAD_DIM)
    padding = jnp.zeros((WINDOW, ATTN_HEADS, HEAD_DIM), jnp.bfloat16)
    seq_keys = jnp.concatenate([padding, keys.reshape(total, ATTN_HEADS, HEAD_DIM)], axis=0)
    seq_values = jnp.concatenate([padding, values.reshape(total, ATTN_HEADS, HEAD_DIM)], axis=0)
    scale = HEAD_DIM ** (-0.5)

    def block(index):
        start = index * WINDOW
        query_part = lax.dynamic_slice_in_dim(seq_queries, start, WINDOW, 0).astype(jnp.float32)
        key_part = lax.dynamic_slice_in_dim(seq_keys, start, 2 * WINDOW, 0).astype(jnp.float32)
        value_part = lax.dynamic_slice_in_dim(seq_values, start, 2 * WINDOW, 0).astype(jnp.float32)
        scores = jnp.einsum('qae,kae->aqk', query_part, key_part) * scale
        query_pos = start + jnp.arange(WINDOW, dtype=jnp.int32)
        key_pos = start - WINDOW + jnp.arange(2 * WINDOW, dtype=jnp.int32)
        offset = query_pos[:, None] - key_pos[None, :]
        allowed = (offset >= 0) & (offset < WINDOW) & (key_pos[None, :] >= 0)
        scores = jnp.where(allowed[None], scores, -1e+30)
        top = lax.optimization_barrier(jnp.max(scores, axis=-1, keepdims=True))
        expo = jnp.exp(scores - top)
        probs = (expo / lax.optimization_barrier(jnp.sum(expo, axis=-1, keepdims=True))).astype(jnp.bfloat16).astype(jnp.float32)
        result = jnp.einsum('aqk,kae->qae', probs, value_part)
        return result.reshape(WINDOW, D)
    pieces = lax.map(block, jnp.arange(total // WINDOW, dtype=jnp.int32))
    return pieces.reshape(GROUPS, GROUP, D)

def reference(queries, keys, values, token_lr, momentum_rate, update_step, fast_weights, momentum):
    attended = attention(queries, keys, values)
    weights = fast_weights
    moment = momentum
    recalls = []
    for index in range(GROUPS):
        half = weights.astype(jnp.bfloat16).astype(jnp.float32)
        gate_w = half[:, 0]
        up_w = half[:, 1]
        down_w = half[:, 2]
        query_unit = unit_rows(queries[index].reshape(GROUP, HEADS, DH)).astype(jnp.bfloat16).astype(jnp.float32)
        key_unit = unit_rows(keys[index].reshape(GROUP, HEADS, DH)).astype(jnp.bfloat16).astype(jnp.float32)
        query_gate = jnp.einsum('lhd,hdf->lhf', query_unit, gate_w)
        query_up = jnp.einsum('lhd,hdf->lhf', query_unit, up_w)
        query_hidden = (jax.nn.silu(query_gate) * query_up).astype(jnp.bfloat16).astype(jnp.float32)
        recalls.append(jnp.einsum('lhf,hfd->lhd', query_hidden, down_w).reshape(GROUP, D))
        key_gate = jnp.einsum('lhd,hdf->lhf', key_unit, gate_w)
        key_up = jnp.einsum('lhd,hdf->lhf', key_unit, up_w)
        key_hidden = (jax.nn.silu(key_gate) * key_up).astype(jnp.bfloat16).astype(jnp.float32)
        rate = jnp.transpose(token_lr[:, index, :])[:, :, None]
        value_heads = values[index].reshape(GROUP, HEADS, DH).astype(jnp.float32)
        target = (-(rate * value_heads)).astype(jnp.bfloat16).astype(jnp.float32)
        back = jnp.einsum('lhd,hfd->lhf', target, down_w)
        sig = jax.nn.sigmoid(key_gate)
        gate_in = (back * key_up * sig * (1.0 + key_gate * (1.0 - sig))).astype(jnp.bfloat16).astype(jnp.float32)
        up_in = (back * jax.nn.silu(key_gate)).astype(jnp.bfloat16).astype(jnp.float32)
        gradient = jnp.stack([jnp.einsum('lhd,lhf->hdf', key_unit, gate_in), jnp.einsum('lhd,lhf->hdf', key_unit, up_in), jnp.einsum('lhf,lhd->hfd', key_hidden, target)], axis=1)
        moment = momentum_rate[:, None, None, None] * moment + gradient
        ortho = (moment * lax.rsqrt(lax.optimization_barrier(jnp.sum(moment * moment, axis=(2, 3), keepdims=True)) + 1e-06)).astype(jnp.bfloat16)
        for turn in range(NS_STEPS):
            wide = ortho.astype(jnp.float32)
            gram = jnp.einsum('hmrd,hmre->hmde', wide, wide)
            ortho = refine(ortho, gram)
        stepped = weights - update_step[:, None, None, None] * ortho.astype(jnp.float32)
        weights = stepped * lax.rsqrt(lax.optimization_barrier(jnp.sum(stepped * stepped, axis=2, keepdims=True)) + 1e-06)
    mixed = (attended + jnp.stack(recalls, axis=0)).astype(jnp.bfloat16)
    return (mixed, weights, moment)
```

```python
import functools

import jax
import jax.numpy as jnp
import numpy as np
from jax import lax
from jax.experimental import pallas as pl
from jax.experimental.pallas import tpu as pltpu
from jax.sharding import PartitionSpec as P

DH = 512
HEAD_DIM = 128
WINDOW = 256
NS_STEPS = 2
GROUPS = 2


quintic_one = 3.4445
quintic_two = -4.775
quintic_three = 2.0315


def shifted(value, axis, steps):
    count = lax.axis_size(axis)
    pairs = [(source, (source + steps) % count) for source in range(count)]
    return lax.ppermute(value, axis, pairs)


def unit_rows(field):
    field = field.astype(jnp.float32)
    return field * lax.rsqrt(jnp.mean(field * field, axis=-1, keepdims=True) + 1e-05)


def refine(ortho, gram):
    gram_half = gram.astype(jnp.bfloat16)
    square = jnp.einsum("hmde,hmef->hmdf", gram_half, gram_half, preferred_element_type=jnp.float32)
    poly = (quintic_two * gram + quintic_three * square).astype(jnp.bfloat16)
    turned = jnp.einsum("hmrd,hmde->hmre", ortho, poly, preferred_element_type=jnp.float32)
    return (quintic_one * ortho.astype(jnp.float32) + turned).astype(jnp.bfloat16)


def sliding_attention(queries, keys, values):
    groups, local_len, local_width = queries.shape
    heads = local_width // HEAD_DIM
    tails = jnp.stack([keys, values], axis=0)
    received = shifted(tails, ("tok", "row"), 1)
    device = lax.axis_index(("tok", "row"))
    earlier = jnp.concatenate([jnp.zeros_like(received[:, :1]), received[:, :-1]], axis=1)
    halo = jnp.where(device == 0, earlier, received)
    ext_keys = jnp.concatenate([halo[0], keys], axis=1)
    ext_values = jnp.concatenate([halo[1], values], axis=1)
    block_len = min(local_len, 512)
    count = local_len // block_len
    group_total = local_len * lax.axis_size(("tok", "row"))
    scale = HEAD_DIM ** (-0.5)
    group_base = jnp.arange(groups, dtype=jnp.int32) * group_total + device * local_len

    def attend(block):
        start = block * block_len
        span = block_len + WINDOW
        query_part = queries.reshape(groups, block_len, heads, HEAD_DIM)
        key_part = ext_keys.reshape(groups, span, heads, HEAD_DIM)
        value_part = ext_values.reshape(groups, span, heads, HEAD_DIM)
        scores = (
            jnp.einsum("cqae,ckae->caqk", query_part, key_part, preferred_element_type=jnp.float32)
            * scale
        )
        query_local = start + jnp.arange(block_len, dtype=jnp.int32)
        key_local = start - WINDOW + jnp.arange(span, dtype=jnp.int32)
        offset = query_local[:, None] - key_local[None, :]
        near = (offset >= 0) & (offset < WINDOW)
        placed = group_base[:, None] + key_local[None, :] >= 0
        allowed = near[None, None, :, :] & placed[:, None, None, :]
        scores = jnp.where(allowed, scores, -1e30)
        top = jnp.max(scores, axis=-1, keepdims=True)
        expo = jnp.exp(scores - top)
        probs = (expo / jnp.sum(expo, axis=-1, keepdims=True)).astype(jnp.bfloat16)
        result = jnp.einsum(
            "caqk,ckae->cqae", probs, value_part, preferred_element_type=jnp.float32
        )
        return result.reshape(groups, block_len, local_width)

    pieces = lax.map(attend, jnp.arange(count, dtype=jnp.int32))
    return jnp.moveaxis(pieces, 0, 1).reshape(groups, local_len, local_width)


def general_shards(queries, keys, values, token_lr, momentum_rate, update_step, fast_weights, momentum):
    attended = sliding_attention(queries, keys, values)
    groups, local_len, local_width = queries.shape
    heads_local = local_width // DH
    query_unit = unit_rows(queries.reshape(groups, local_len, heads_local, DH)).astype(jnp.bfloat16)
    key_unit = unit_rows(keys.reshape(groups, local_len, heads_local, DH)).astype(jnp.bfloat16)
    value_heads = values.reshape(groups, local_len, heads_local, DH)
    rows = fast_weights.shape[2]
    row_start = lax.axis_index("row") * rows
    weights = fast_weights
    moment = momentum
    recalls = []
    for index in range(GROUPS):
        half = lax.all_gather(weights.astype(jnp.bfloat16), "row", axis=2, tiled=True)
        gate_w = half[:, 0]
        up_w = half[:, 1]
        down_w = half[:, 2]
        query_gate = jnp.einsum(
            "lhd,hdf->lhf", query_unit[index], gate_w, preferred_element_type=jnp.float32
        )
        query_up = jnp.einsum(
            "lhd,hdf->lhf", query_unit[index], up_w, preferred_element_type=jnp.float32
        )
        query_hidden = (jax.nn.silu(query_gate) * query_up).astype(jnp.bfloat16)
        recall = jnp.einsum(
            "lhf,hfd->lhd", query_hidden, down_w, preferred_element_type=jnp.float32
        )
        recalls.append(recall.reshape(local_len, local_width))
        key_gate = jnp.einsum(
            "lhd,hdf->lhf", key_unit[index], gate_w, preferred_element_type=jnp.float32
        )
        key_up = jnp.einsum(
            "lhd,hdf->lhf", key_unit[index], up_w, preferred_element_type=jnp.float32
        )
        key_hidden = (jax.nn.silu(key_gate) * key_up).astype(jnp.bfloat16)
        rate = jnp.transpose(token_lr[:, index, :])[:, :, None]
        target = (-(rate * value_heads[index].astype(jnp.float32))).astype(jnp.bfloat16)
        back = jnp.einsum("lhd,hfd->lhf", target, down_w, preferred_element_type=jnp.float32)
        sig = jax.nn.sigmoid(key_gate)
        gate_in = (back * key_up * sig * (1.0 + key_gate * (1.0 - sig))).astype(jnp.bfloat16)
        up_in = (back * jax.nn.silu(key_gate)).astype(jnp.bfloat16)
        gradient = jnp.stack(
            [
                jnp.einsum(
                    "lhd,lhf->hdf", key_unit[index], gate_in, preferred_element_type=jnp.float32
                ),
                jnp.einsum(
                    "lhd,lhf->hdf", key_unit[index], up_in, preferred_element_type=jnp.float32
                ),
                jnp.einsum("lhf,lhd->hfd", key_hidden, target, preferred_element_type=jnp.float32),
            ],
            axis=1,
        )
        halves = lax.psum_scatter(
            gradient.astype(jnp.bfloat16), "row", scatter_dimension=2, tiled=True
        )
        owned = lax.psum(halves, "tok").astype(jnp.float32)
        moment = momentum_rate[:, None, None, None] * moment + owned
        whole = lax.all_gather(moment.astype(jnp.bfloat16), "row", axis=2, tiled=True).astype(
            moment.dtype
        )
        ortho = (
            whole * lax.rsqrt(jnp.sum(whole * whole, axis=(2, 3), keepdims=True) + 1e-06)
        ).astype(jnp.bfloat16)
        for turn in range(NS_STEPS):
            gram = jnp.einsum("hmrd,hmre->hmde", ortho, ortho, preferred_element_type=jnp.float32)
            ortho = refine(ortho, gram)
        ortho = lax.dynamic_slice_in_dim(ortho, row_start, rows, 2)
        stepped = weights - update_step[:, None, None, None] * ortho.astype(jnp.float32)
        columns = lax.psum(jnp.sum(stepped * stepped, axis=2), "row")
        weights = stepped * lax.rsqrt(columns[:, :, None, :] + 1e-06)
    mixed = (attended + jnp.stack(recalls, axis=0)).astype(jnp.bfloat16)
    return (mixed, weights, moment)


F32 = jnp.float32
BF16 = jnp.bfloat16
VMEM_LIMIT = 48 * 1024 * 1024


def dot(a, b):
    return lax.dot_general(a, b, (((1,), (0,)), ((), ())), preferred_element_type=F32)


def dot_tn(a, b):
    return lax.dot_general(a, b, (((0,), (0,)), ((), ())), preferred_element_type=F32)


def dot_nt(a, b):
    return lax.dot_general(a, b, (((1,), (1,)), ((), ())), preferred_element_type=F32)


def unit(field):
    field = field.astype(F32)
    mean = jnp.mean(field * field, axis=-1, keepdims=True)
    return (field * lax.rsqrt(mean + 1e-05)).astype(BF16)


def sigmoid(value):
    return 1.0 / (1.0 + jnp.exp(-value))


def params(**more):
    return pltpu.CompilerParams(vmem_limit_bytes=VMEM_LIMIT, **more)


def cost(flops, moved):
    return pl.CostEstimate(flops=int(flops), bytes_accessed=int(moved), transcendentals=0)


def prep_body(info, keys, values, rates, *outs):
    rate_all = rates[0]
    lanes = lax.broadcasted_iota(jnp.int32, rate_all.shape, 1)
    width = outs[0].shape[-1]
    for slot, out in enumerate(outs):
        head = info[0] ^ slot
        columns = pl.ds(pl.multiple_of(head * width, width), width)
        out[0] = unit(keys[0, :, columns])
        rate = jnp.sum(jnp.where(lanes == head, rate_all, 0.0), axis=1, keepdims=True)
        out[1] = (-(rate * values[0, :, columns].astype(F32))).astype(BF16)


def prep(block, info, keys, values, rates):
    _, length, width = keys.shape
    heads = rates.shape[-1]
    each = jax.ShapeDtypeStruct((2, length, width // heads), BF16)
    return pl.pallas_call(
        prep_body,
        grid_spec=pltpu.PrefetchScalarGridSpec(
            num_scalar_prefetch=1,
            grid=(1,),
            in_specs=[
                pl.BlockSpec((1, length, width), lambda i, info: (block, 0, 0)),
                pl.BlockSpec((1, length, width), lambda i, info: (block, 0, 0)),
                pl.BlockSpec((1, length, heads), lambda i, info: (block, 0, 0)),
            ],
            out_specs=[pl.BlockSpec(each.shape, lambda i, info: (0, 0, 0))] * heads,
        ),
        out_shape=[each] * heads,
        compiler_params=params(),
        cost_estimate=cost(0, 8 * length * width),
        name="prep",
    )(info, keys, values, rates)


def place_halves(info, target, own, other):
    rows = own.shape[0]
    target[pl.ds(pl.multiple_of(info[1] * rows, rows), rows), :] = own.astype(BF16)
    target[pl.ds(pl.multiple_of((1 - info[1]) * rows, rows), rows), :] = other.astype(BF16)


def grad_body(slots, info, *refs):
    parts = refs[:slots]
    own, other, out, weights, units, targets, hidden, gates, ups = refs[slots:]
    length = parts[0].shape[1]
    for matrix in range(3):
        place_halves(info, weights.at[matrix], own[0, matrix], other[0, matrix])
    for slot, part in enumerate(parts):
        span = pl.ds(slot * length, length)
        key_unit = part[0]
        target = part[1]
        units[span, :] = key_unit
        targets[span, :] = target
        key_gate = dot(key_unit, weights[0])
        key_up = dot(key_unit, weights[1])
        back = dot_nt(target, weights[2])
        sig = sigmoid(key_gate)
        silu = key_gate * sig
        hidden[span, :] = (silu * key_up).astype(BF16)
        gates[span, :] = (back * key_up * sig * (1.0 + key_gate * (1.0 - sig))).astype(BF16)
        ups[span, :] = (back * silu).astype(BF16)
    rows = own.shape[2]
    for half in range(2):
        place = info[1] if half == 0 else 1 - info[1]
        columns = pl.ds(pl.multiple_of(place * rows, rows), rows)
        out[half, 0] = dot_tn(units[:, columns], gates[...]).astype(BF16)
        out[half, 1] = dot_tn(units[:, columns], ups[...]).astype(BF16)
        out[half, 2] = dot_tn(hidden[:, columns], targets[...]).astype(BF16)


def head_spec(shape):
    alone = shape[0] == 1
    return pl.BlockSpec((1,) + shape[1:], lambda i, info: (0 if alone else info[0], 0, 0, 0))


def grad(info, parts, own, other):
    slots = len(parts)
    _, length, width = parts[0].shape
    rows = own.shape[2]
    total = slots * length
    return pl.pallas_call(
        functools.partial(grad_body, slots),
        grid_spec=pltpu.PrefetchScalarGridSpec(
            num_scalar_prefetch=1,
            grid=(1,),
            in_specs=[pl.BlockSpec((2, length, width), lambda i, info: (0, 0, 0))] * slots
            + [head_spec(own.shape)] * 2,
            out_specs=pl.BlockSpec((2, 3, rows, width), lambda i, info: (0, 0, 0, 0)),
            scratch_shapes=[pltpu.VMEM((3, width, width), BF16)]
            + [pltpu.VMEM((total, width), BF16)] * 5,
        ),
        out_shape=jax.ShapeDtypeStruct((2, 3, rows, width), BF16),
        compiler_params=params(),
        cost_estimate=cost(12 * total * width * width, 4 * total * width + 15 * width * width),
        name="grad",
    )(info, *parts, own, other)


def polish(ortho):
    gram = dot_tn(ortho, ortho)
    gram_half = gram.astype(BF16)
    square = dot(gram_half, gram_half)
    poly = (quintic_two * gram + quintic_three * square).astype(BF16)
    return (quintic_one * ortho.astype(F32) + dot(ortho, poly)).astype(BF16)


def update_body(summed, last, kept, info, rate, step, ga, gb, m_own, m_oth, w_own, w_oth, *refs):
    refs = refs[kept:]
    if last:
        m_out, w_out = refs[:2]
        refs = refs[2:]
    else:
        m_out, mo_out, w_out, wo_out = refs[:4]
        refs = refs[4:]
    head = info[0]
    alone = []
    if summed:
        g_out, *alone, g_own, g_oth = refs
        g_own[...] = (ga[0, 0].astype(F32) + gb[1, 0].astype(F32)).astype(BF16)
        g_oth[...] = (ga[1, 0].astype(F32) + gb[0, 0].astype(F32)).astype(BF16)
        g_out[0] = g_own[...]
        grad_own = g_own[...].astype(F32)
        grad_oth = g_oth[...].astype(F32)
    else:
        grad_own = ga[0].astype(F32)
        grad_oth = gb[0].astype(F32)
    moment_own = rate[head] * m_own[0, 0] + grad_own
    moment_oth = rate[head] * m_oth[0, 0] + grad_oth
    m_out[0, 0] = moment_own
    if not last:
        mo_out[0, 0] = moment_oth
    power = jnp.sum(moment_own * moment_own + moment_oth * moment_oth, keepdims=True)
    scale = lax.rsqrt(power + 1e-06)
    ortho = jnp.concatenate(
        [(moment_own * scale).astype(BF16), (moment_oth * scale).astype(BF16)], axis=0
    )
    for turn in range(NS_STEPS):
        ortho = polish(ortho)
    rows = m_own.shape[2]
    stepped_own = w_own[0, 0] - step[head] * ortho[:rows].astype(F32)
    stepped_oth = w_oth[0, 0] - step[head] * ortho[rows:].astype(F32)
    columns = jnp.sum(stepped_own * stepped_own + stepped_oth * stepped_oth, axis=0, keepdims=True)
    scale = lax.rsqrt(columns + 1e-06)
    w_out[0, 0] = stepped_own * scale
    if not last:
        wo_out[0, 0] = stepped_oth * scale
    if alone:
        alone[0][0, 0] = moment_own
        alone[1][0, 0] = moment_oth
        alone[2][0, 0] = stepped_own * scale
        alone[3][0, 0] = stepped_oth * scale


def update(info, rate, step, ga, gb, state, previous, summed, last):
    _, _, rows, width = state[0].shape
    heads = rate.shape[0]
    block = pl.BlockSpec((1, 1, rows, width), lambda m, info: (info[0], m, 0, 0))
    alone = pl.BlockSpec((1, 1, rows, width), lambda m, info: (0, m, 0, 0))
    scalars = pl.BlockSpec(memory_space=pltpu.SMEM)
    if summed:
        g_spec = pl.BlockSpec((2, 1, rows, width), lambda m, info: (0, m, 0, 0))
    else:
        g_spec = pl.BlockSpec((1, rows, width), lambda m, info: (m, 0, 0))
    whole = jax.ShapeDtypeStruct((heads, 3, rows, width), F32)
    count = 2 if last else 4
    out_shape = [whole] * count
    out_specs = [block] * count
    scratch = []
    if summed:
        out_shape.append(jax.ShapeDtypeStruct((3, rows, width), BF16))
        out_specs.append(pl.BlockSpec((1, rows, width), lambda m, info: (m, 0, 0)))
        if not last:
            out_shape += [jax.ShapeDtypeStruct((1, 3, rows, width), F32)] * 4
            out_specs += [alone] * 4
        scratch = [pltpu.VMEM((rows, width), BF16)] * 2
    kept = 0 if previous is None else count
    return pl.pallas_call(
        functools.partial(update_body, summed, last, kept),
        grid_spec=pltpu.PrefetchScalarGridSpec(
            num_scalar_prefetch=1,
            grid=(3,),
            in_specs=[scalars] * 2 + [g_spec] * 2
            + [block if value.shape[0] == heads else alone for value in state]
            + [pl.BlockSpec(memory_space=pl.ANY)] * kept,
            out_specs=out_specs,
            scratch_shapes=scratch,
        ),
        out_shape=out_shape,
        input_output_aliases={9 + i: i for i in range(kept)},
        compiler_params=params(),
        cost_estimate=cost(3 * 6 * 2 * width**3, 3 * 16 * rows * width),
        name="update",
    )(info, rate, step, ga, gb, *state, *(previous or []))


def mix_body(block, kept, info, queries, keys, values, early_k, early_v, own, other, *refs):
    out, weights = refs[kept:]
    length, width = queries.shape[1:]
    for matrix in range(3):
        place_halves(info, weights.at[matrix], own[0, matrix], other[0, matrix])
    query_unit = unit(queries[0])
    gate = dot(query_unit, weights[0])
    hidden = (gate * sigmoid(gate) * dot(query_unit, weights[1])).astype(BF16)
    recall = dot(hidden, weights[2])
    rows = lax.broadcasted_iota(jnp.int32, (length, length), 0)
    lanes = lax.broadcasted_iota(jnp.int32, (length, length), 1)
    here = lanes <= rows
    factor = HEAD_DIM ** (-0.5) * float(np.log2(np.e))
    for head in range(width // HEAD_DIM):
        columns = slice(head * HEAD_DIM, (head + 1) * HEAD_DIM)
        query = queries[0, :, columns]
        late = dot_nt(query, keys[0, :, columns])
        early = dot_nt(query, early_k[0, :, columns])
        if block == 0:
            early = early + jnp.where(info[2] == 1, -1e30, 0.0)
        scores = jnp.where(here, late, early)
        top = jnp.max(scores, axis=1, keepdims=True)
        expo = jnp.exp2((scores - top) * factor)
        total = jnp.sum(expo, axis=1, keepdims=True)
        result = dot(jnp.where(here, expo, 0.0).astype(BF16), values[0, :, columns])
        result += dot(jnp.where(here, 0.0, expo).astype(BF16), early_v[0, :, columns])
        out[0, :, columns] = (result * (1.0 / total) + recall[:, columns]).astype(BF16)


def mix(block, info, queries, keys, values, early_k, early_v, own, other, previous):
    groups, length, width = queries.shape
    heads = own.shape[0]
    part = width // heads
    here = pl.BlockSpec((1, length, part), lambda h, info: (block, 0, h))
    if block:
        before = pl.BlockSpec((1, length, part), lambda h, info: (block - info[2], 0, h))
    else:
        before = here
    weight = pl.BlockSpec((1,) + own.shape[1:], lambda h, info: (h, 0, 0, 0))
    kept = [] if previous is None else [previous]
    return pl.pallas_call(
        functools.partial(mix_body, block, len(kept)),
        grid_spec=pltpu.PrefetchScalarGridSpec(
            num_scalar_prefetch=1,
            grid=(heads,),
            in_specs=[here] * 3 + [before] * 2 + [weight] * 2
            + [pl.BlockSpec(memory_space=pl.ANY)] * len(kept),
            out_specs=here,
            scratch_shapes=[pltpu.VMEM((3, part, part), BF16)],
        ),
        out_shape=jax.ShapeDtypeStruct(queries.shape, BF16),
        input_output_aliases={8: 0} if kept else {},
        compiler_params=params(),
        cost_estimate=cost(
            heads * (6 * length * part * part + 8 * length * length * part),
            12 * length * width + 12 * width * part,
        ),
        name="mix",
    )(info, queries, keys, values, early_k, early_v, own, other, *kept)


def owner_shards(queries, keys, values, token_lr, momentum_rate, update_step, fast_weights, momentum):
    groups, length, _ = queries.shape
    chips = lax.axis_size("tok")
    chip = lax.axis_index("tok")
    row = lax.axis_index("row")
    first = (lax.axis_index(("tok", "row")) == 0).astype(jnp.int32)
    infos = [jnp.stack([chip ^ slot, row, first]).astype(jnp.int32) for slot in range(chips)]
    rates = jnp.transpose(token_lr, (1, 2, 0))

    def to_chip(value, slot):
        return lax.ppermute(value, "tok", [(c, c ^ slot) for c in range(chips)])

    def to_core(value):
        return lax.ppermute(value, "row", [(0, 1), (1, 0)])

    early_k = shifted(keys, ("tok", "row"), 1)
    early_v = shifted(values, ("tok", "row"), 1)
    w_own, m_own = fast_weights, momentum
    w_oth, m_oth = to_core(fast_weights), to_core(momentum)
    parts = []
    for block in range(groups):
        sent = prep(block, infos[0], keys, values, rates)
        parts.append([sent[0]] + [to_chip(sent[slot], slot) for slot in range(1, chips)])
    mixed = None
    alone = (m_own, m_oth, w_own, w_oth)
    for block in range(groups):
        last = block == groups - 1
        partial = grad(infos[0], parts[block], alone[2], alone[3])
        state = (m_own, m_oth, w_own, w_oth)
        results = update(
            infos[0], momentum_rate, update_step, partial, to_core(partial), alone, None, True, last
        )
        count = 2 if last else 4
        after, gradient, alone = results[:count], results[count], results[count + 1 :]
        mixed = mix(
            block, infos[0], queries, keys, values, early_k, early_v, w_own, w_oth, mixed
        )
        for slot in range(1, chips):
            arrived = to_chip(gradient, slot)
            after = update(
                infos[slot], momentum_rate, update_step, arrived, to_core(arrived), state, after,
                False, last,
            )
        if last:
            m_own, w_own = after
        else:
            m_own, m_oth, w_own, w_oth = after
    return (mixed, w_own, m_own)


def shards(chips, queries, *rest):
    heads = queries.shape[2] // DH
    if heads == chips and chips & (chips - 1) == 0 and queries.shape[1] == WINDOW:
        return owner_shards(queries, *rest)
    return general_shards(queries, *rest)


def solution(mesh):
    return jax.shard_map(
        functools.partial(shards, mesh.shape["tok"]),
        mesh=mesh,
        in_specs=(
            P(None, ("tok", "row"), "mem"),
            P(None, ("tok", "row"), "mem"),
            P(None, ("tok", "row"), "mem"),
            P("mem", None, ("tok", "row")),
            P("mem"),
            P("mem"),
            P("mem", None, "row", None),
            P("mem", None, "row", None),
        ),
        out_specs=(
            P(None, ("tok", "row"), "mem"),
            P("mem", None, "row", None),
            P("mem", None, "row", None),
        ),
        check_vma=False,
    )
```

```python
import functools

import jax
import jax.numpy as jnp
import numpy as np
from jax import lax
from jax.experimental import pallas as pl
from jax.experimental.pallas import tpu as pltpu
from jax.sharding import PartitionSpec as P

DH = 512
HEAD_DIM = 128
WINDOW = 256
NS_STEPS = 2
GROUPS = 2


quintic_one = 3.4445
quintic_two = -4.775
quintic_three = 2.0315


def shifted(value, axis, steps):
    count = lax.axis_size(axis)
    pairs = [(source, (source + steps) % count) for source in range(count)]
    return lax.ppermute(value, axis, pairs)


def unit_rows(field):
    field = field.astype(jnp.float32)
    return field * lax.rsqrt(jnp.mean(field * field, axis=-1, keepdims=True) + 1e-05)


def refine(ortho, gram):
    gram_half = gram.astype(jnp.bfloat16)
    square = jnp.einsum("hmde,hmef->hmdf", gram_half, gram_half, preferred_element_type=jnp.float32)
    poly = (quintic_two * gram + quintic_three * square).astype(jnp.bfloat16)
    turned = jnp.einsum("hmrd,hmde->hmre", ortho, poly, preferred_element_type=jnp.float32)
    return (quintic_one * ortho.astype(jnp.float32) + turned).astype(jnp.bfloat16)


def sliding_attention(queries, keys, values):
    groups, local_len, local_width = queries.shape
    heads = local_width // HEAD_DIM
    tails = jnp.stack([keys, values], axis=0)
    received = shifted(tails, ("tok", "row"), 1)
    device = lax.axis_index(("tok", "row"))
    earlier = jnp.concatenate([jnp.zeros_like(received[:, :1]), received[:, :-1]], axis=1)
    halo = jnp.where(device == 0, earlier, received)
    ext_keys = jnp.concatenate([halo[0], keys], axis=1)
    ext_values = jnp.concatenate([halo[1], values], axis=1)
    block_len = min(local_len, 512)
    count = local_len // block_len
    group_total = local_len * lax.axis_size(("tok", "row"))
    scale = HEAD_DIM ** (-0.5)
    group_base = jnp.arange(groups, dtype=jnp.int32) * group_total + device * local_len

    def attend(block):
        start = block * block_len
        span = block_len + WINDOW
        query_part = queries.reshape(groups, block_len, heads, HEAD_DIM)
        key_part = ext_keys.reshape(groups, span, heads, HEAD_DIM)
        value_part = ext_values.reshape(groups, span, heads, HEAD_DIM)
        scores = (
            jnp.einsum("cqae,ckae->caqk", query_part, key_part, preferred_element_type=jnp.float32)
            * scale
        )
        query_local = start + jnp.arange(block_len, dtype=jnp.int32)
        key_local = start - WINDOW + jnp.arange(span, dtype=jnp.int32)
        offset = query_local[:, None] - key_local[None, :]
        near = (offset >= 0) & (offset < WINDOW)
        placed = group_base[:, None] + key_local[None, :] >= 0
        allowed = near[None, None, :, :] & placed[:, None, None, :]
        scores = jnp.where(allowed, scores, -1e30)
        top = jnp.max(scores, axis=-1, keepdims=True)
        expo = jnp.exp(scores - top)
        probs = (expo / jnp.sum(expo, axis=-1, keepdims=True)).astype(jnp.bfloat16)
        result = jnp.einsum(
            "caqk,ckae->cqae", probs, value_part, preferred_element_type=jnp.float32
        )
        return result.reshape(groups, block_len, local_width)

    pieces = lax.map(attend, jnp.arange(count, dtype=jnp.int32))
    return jnp.moveaxis(pieces, 0, 1).reshape(groups, local_len, local_width)


def general_shards(queries, keys, values, token_lr, momentum_rate, update_step, fast_weights, momentum):
    attended = sliding_attention(queries, keys, values)
    groups, local_len, local_width = queries.shape
    heads_local = local_width // DH
    query_unit = unit_rows(queries.reshape(groups, local_len, heads_local, DH)).astype(jnp.bfloat16)
    key_unit = unit_rows(keys.reshape(groups, local_len, heads_local, DH)).astype(jnp.bfloat16)
    value_heads = values.reshape(groups, local_len, heads_local, DH)
    rows = fast_weights.shape[2]
    row_start = lax.axis_index("row") * rows
    weights = fast_weights
    moment = momentum
    recalls = []
    for index in range(GROUPS):
        half = lax.all_gather(weights.astype(jnp.bfloat16), "row", axis=2, tiled=True)
        gate_w = half[:, 0]
        up_w = half[:, 1]
        down_w = half[:, 2]
        query_gate = jnp.einsum(
            "lhd,hdf->lhf", query_unit[index], gate_w, preferred_element_type=jnp.float32
        )
        query_up = jnp.einsum(
            "lhd,hdf->lhf", query_unit[index], up_w, preferred_element_type=jnp.float32
        )
        query_hidden = (jax.nn.silu(query_gate) * query_up).astype(jnp.bfloat16)
        recall = jnp.einsum(
            "lhf,hfd->lhd", query_hidden, down_w, preferred_element_type=jnp.float32
        )
        recalls.append(recall.reshape(local_len, local_width))
        key_gate = jnp.einsum(
            "lhd,hdf->lhf", key_unit[index], gate_w, preferred_element_type=jnp.float32
        )
        key_up = jnp.einsum(
            "lhd,hdf->lhf", key_unit[index], up_w, preferred_element_type=jnp.float32
        )
        key_hidden = (jax.nn.silu(key_gate) * key_up).astype(jnp.bfloat16)
        rate = jnp.transpose(token_lr[:, index, :])[:, :, None]
        target = (-(rate * value_heads[index].astype(jnp.float32))).astype(jnp.bfloat16)
        back = jnp.einsum("lhd,hfd->lhf", target, down_w, preferred_element_type=jnp.float32)
        sig = jax.nn.sigmoid(key_gate)
        gate_in = (back * key_up * sig * (1.0 + key_gate * (1.0 - sig))).astype(jnp.bfloat16)
        up_in = (back * jax.nn.silu(key_gate)).astype(jnp.bfloat16)
        gradient = jnp.stack(
            [
                jnp.einsum(
                    "lhd,lhf->hdf", key_unit[index], gate_in, preferred_element_type=jnp.float32
                ),
                jnp.einsum(
                    "lhd,lhf->hdf", key_unit[index], up_in, preferred_element_type=jnp.float32
                ),
                jnp.einsum("lhf,lhd->hfd", key_hidden, target, preferred_element_type=jnp.float32),
            ],
            axis=1,
        )
        halves = lax.psum_scatter(
            gradient.astype(jnp.bfloat16), "row", scatter_dimension=2, tiled=True
        )
        owned = lax.psum(halves, "tok").astype(jnp.float32)
        moment = momentum_rate[:, None, None, None] * moment + owned
        whole = lax.all_gather(moment.astype(jnp.bfloat16), "row", axis=2, tiled=True).astype(
            moment.dtype
        )
        ortho = (
            whole * lax.rsqrt(jnp.sum(whole * whole, axis=(2, 3), keepdims=True) + 1e-06)
        ).astype(jnp.bfloat16)
        for turn in range(NS_STEPS):
            gram = jnp.einsum("hmrd,hmre->hmde", ortho, ortho, preferred_element_type=jnp.float32)
            ortho = refine(ortho, gram)
        ortho = lax.dynamic_slice_in_dim(ortho, row_start, rows, 2)
        stepped = weights - update_step[:, None, None, None] * ortho.astype(jnp.float32)
        columns = lax.psum(jnp.sum(stepped * stepped, axis=2), "row")
        weights = stepped * lax.rsqrt(columns[:, :, None, :] + 1e-06)
    mixed = (attended + jnp.stack(recalls, axis=0)).astype(jnp.bfloat16)
    return (mixed, weights, moment)


F32 = jnp.float32
BF16 = jnp.bfloat16
SHARE = 0.05
VMEM_LIMIT = 48 * 1024 * 1024


def dot(a, b):
    return lax.dot_general(a, b, (((1,), (0,)), ((), ())), preferred_element_type=F32)


def dot_tn(a, b):
    return lax.dot_general(a, b, (((0,), (0,)), ((), ())), preferred_element_type=F32)


def dot_nt(a, b):
    return lax.dot_general(a, b, (((1,), (1,)), ((), ())), preferred_element_type=F32)


def unit(field):
    field = field.astype(F32)
    mean = jnp.mean(field * field, axis=-1, keepdims=True)
    return (field * lax.rsqrt(mean + 1e-05)).astype(BF16)


def sigmoid(value):
    return 1.0 / (1.0 + jnp.exp(-value))


def params(**more):
    return pltpu.CompilerParams(vmem_limit_bytes=VMEM_LIMIT, **more)


def cost(flops, moved):
    return pl.CostEstimate(flops=int(flops * SHARE), bytes_accessed=int(moved * SHARE), transcendentals=0)


INFO = jax.ShapeDtypeStruct((3,), jnp.int32)


def hand_on(info, info_out):
    for i in range(info.shape[0]):
        info_out[i] = info[i]


def prep_body(groups, info, keys, values, rates, *outs):
    sends, tails, info_out = outs[: -groups - 1], outs[-groups - 1 : -1], outs[-1]
    hand_on(info, info_out)
    for group, tail in enumerate(tails):

        @pl.when(pl.program_id(0) == group)
        def _():
            tail[0] = keys[0]
            tail[1] = values[0]

    rate_all = rates[0]
    lanes = lax.broadcasted_iota(jnp.int32, rate_all.shape, 1)
    width = sends[0].shape[-1]
    for slot, out in enumerate(sends):
        head = info[0] ^ slot
        columns = pl.ds(pl.multiple_of(head * width, width), width)
        out[0, 0] = unit(keys[0, :, columns])
        rate = jnp.sum(jnp.where(lanes == head, rate_all, 0.0), axis=1, keepdims=True)
        out[0, 1] = (-(rate * values[0, :, columns].astype(F32))).astype(BF16)


def prep(info, keys, values, rates):
    groups, length, width = keys.shape
    heads = rates.shape[-1]
    part = width // heads
    return pl.pallas_call(
        functools.partial(prep_body, groups),
        grid_spec=pltpu.PrefetchScalarGridSpec(
            num_scalar_prefetch=1,
            grid=(groups,),
            in_specs=[
                pl.BlockSpec((1, length, width), lambda i, info: (i, 0, 0)),
                pl.BlockSpec((1, length, width), lambda i, info: (i, 0, 0)),
                pl.BlockSpec((1, length, heads), lambda i, info: (i, 0, 0)),
            ],
            out_specs=[pl.BlockSpec((1, 2, length, part), lambda i, info: (i, 0, 0, 0))] * heads
            + [pl.BlockSpec((2, length, width), lambda i, info: (0, 0, 0))] * groups
            + [pl.BlockSpec(memory_space=pltpu.SMEM)],
        ),
        out_shape=[jax.ShapeDtypeStruct((groups, 2, length, part), BF16)] * heads
        + [jax.ShapeDtypeStruct((2, length, width), BF16)] * groups
        + [INFO],
        compiler_params=params(),
        cost_estimate=cost(0, 12 * groups * length * width),
        name="prep",
    )(info, keys, values, rates)


def place_halves(info, target, own, other):
    rows = own.shape[0]
    target[pl.ds(pl.multiple_of(info[1] * rows, rows), rows), :] = own.astype(BF16)
    target[pl.ds(pl.multiple_of((1 - info[1]) * rows, rows), rows), :] = other.astype(BF16)


def grad_body(slots, info, *refs):
    parts = refs[:slots]
    own, other, out, info_out, weights, units, targets, hidden, gates, ups = refs[slots:]
    hand_on(info, info_out)
    length = parts[0].shape[2]
    for matrix in range(3):
        place_halves(info, weights.at[matrix], own[0, matrix], other[0, matrix])
    for slot, part in enumerate(parts):
        span = pl.ds(slot * length, length)
        key_unit = part[0, 0]
        target = part[0, 1]
        units[span, :] = key_unit
        targets[span, :] = target
        key_gate = dot(key_unit, weights[0])
        key_up = dot(key_unit, weights[1])
        back = dot_nt(target, weights[2])
        sig = sigmoid(key_gate)
        silu = key_gate * sig
        hidden[span, :] = (silu * key_up).astype(BF16)
        gates[span, :] = (back * key_up * sig * (1.0 + key_gate * (1.0 - sig))).astype(BF16)
        ups[span, :] = (back * silu).astype(BF16)
    rows = own.shape[2]
    for half in range(2):
        place = info[1] if half == 0 else 1 - info[1]
        columns = pl.ds(pl.multiple_of(place * rows, rows), rows)
        out[half, 0] = dot_tn(units[:, columns], gates[...]).astype(BF16)
        out[half, 1] = dot_tn(units[:, columns], ups[...]).astype(BF16)
        out[half, 2] = dot_tn(hidden[:, columns], targets[...]).astype(BF16)


def head_spec(shape):
    alone = shape[0] == 1
    return pl.BlockSpec((1,) + shape[1:], lambda i, info: (0 if alone else info[0], 0, 0, 0))


def grad(block, info, parts, own, other):
    slots = len(parts)
    _, _, length, width = parts[0].shape
    rows = own.shape[2]
    total = slots * length
    return pl.pallas_call(
        functools.partial(grad_body, slots),
        grid_spec=pltpu.PrefetchScalarGridSpec(
            num_scalar_prefetch=1,
            grid=(1,),
            in_specs=[pl.BlockSpec((1, 2, length, width), lambda i, info: (block, 0, 0, 0))] * slots
            + [head_spec(own.shape)] * 2,
            out_specs=[
                pl.BlockSpec((2, 3, rows, width), lambda i, info: (0, 0, 0, 0)),
                pl.BlockSpec(memory_space=pltpu.SMEM),
            ],
            scratch_shapes=[pltpu.VMEM((3, width, width), BF16)]
            + [pltpu.VMEM((total, width), BF16)] * 5,
        ),
        out_shape=[jax.ShapeDtypeStruct((2, 3, rows, width), BF16), INFO],
        compiler_params=params(),
        cost_estimate=cost(12 * total * width * width, 4 * total * width + 15 * width * width),
        name="grad",
    )(info, *parts, own, other)


OWN_SKEW = 2
REST_SKEW = 2


def stages(rate, step, gradient, moment, weight, save):
    held = {}

    def begin():
        own, oth = (rate * old() + new() for old, new in zip(moment, gradient))
        save("moment", own, oth)
        power = jnp.sum(own * own + oth * oth, keepdims=True)
        scale = lax.rsqrt(power + 1e-06)
        held["x"] = jnp.concatenate([(own * scale).astype(BF16), (oth * scale).astype(BF16)], axis=0)

    def gram():
        held["gram"] = dot_tn(held["x"], held["x"])

    def poly():
        half = held["gram"].astype(BF16)
        held["poly"] = (quintic_two * held["gram"] + quintic_three * dot(half, half)).astype(BF16)

    def turn():
        turned = quintic_one * held["x"].astype(F32) + dot(held["x"], held["poly"])
        held["x"] = turned.astype(BF16)

    def finish():
        rows = held["x"].shape[0] // 2
        own = weight[0]() - step * held["x"][:rows].astype(F32)
        oth = weight[1]() - step * held["x"][rows:].astype(F32)
        columns = jnp.sum(own * own + oth * oth, axis=0, keepdims=True)
        scale = lax.rsqrt(columns + 1e-06)
        save("weight", own * scale, oth * scale)

    return [begin] + [gram, poly, turn] * NS_STEPS + [finish]


def interleave(work, skew):
    for now in range(len(work[0]) + skew * (len(work) - 1)):
        for place, steps in enumerate(work):
            if 0 <= now - skew * place < len(steps):
                steps[now - skew * place]()


def own_body(last, whole, info, rate, step, mine, theirs, *refs):
    state = refs[:4]
    count = 2 if last else 4
    outs = refs[4 : 4 + count]
    g_out, info_out, moments, weights, m_half, w_half, load_sem, save_sem = refs[4 + count :]
    hand_on(info, info_out)
    head = info[0]
    matrices, rows, _ = g_out.shape
    if whole:
        homes = [moments.at[0], moments.at[1], weights.at[0], weights.at[1]]
    else:
        homes = [moments.at[0], m_half, weights.at[0], w_half]
    source = head if whole else 0
    loads = [
        [
            pltpu.make_async_copy(state[i].at[source, j], homes[i].at[j], load_sem.at[i, j])
            for j in range(matrices)
        ]
        for i in range(4)
    ]
    for i in range(4):
        for load in loads[i]:
            load.start()
    target = head if last else 0
    sources = [moments.at[0], weights.at[0]] if last else [moments.at[0], m_half, weights.at[0], w_half]
    saves = [
        [
            pltpu.make_async_copy(sources[i].at[j], outs[i].at[target, j], save_sem.at[i, j])
            for j in range(matrices)
        ]
        for i in range(count)
    ]
    for j in range(matrices):
        g_out[j] = (mine[0, j].astype(F32) + theirs[1, j].astype(F32)).astype(BF16)

    def plan(j):
        def moment(i):
            loads[i][j].wait()
            return homes[i][j].astype(F32)

        def other_gradient():
            total = mine[1, j].astype(F32) + theirs[0, j].astype(F32)
            return total.astype(BF16).astype(F32)

        def save(kind, own, oth):
            first = 0 if kind == "moment" else count // 2
            keep, half = (moments, m_half) if kind == "moment" else (weights, w_half)
            keep[0, j] = own
            if not last:
                half[j] = oth.astype(BF16)
            for i in range(first, first + count // 2):
                saves[i][j].start()

        return stages(
            rate[head], step[head],
            (lambda: g_out[j].astype(F32), other_gradient),
            (lambda: moment(0), lambda: moment(1)),
            (lambda: moment(2), lambda: moment(3)),
            save,
        )

    interleave([plan(j) for j in range(matrices)], OWN_SKEW)
    for group in saves:
        for save in group:
            save.wait()


def own_update(info, rate, step, mine, theirs, state, last):
    _, matrices, rows, width = state[0].shape
    heads = rate.shape[0]
    whole = state[0].shape[0] == heads
    scalars = pl.BlockSpec(memory_space=pltpu.SMEM)
    near = pl.BlockSpec(memory_space=pltpu.VMEM)
    far = pl.BlockSpec(memory_space=pltpu.HBM)
    full = jax.ShapeDtypeStruct((heads, matrices, rows, width), F32)
    one = jax.ShapeDtypeStruct((1, matrices, rows, width), F32)
    half = jax.ShapeDtypeStruct((1, matrices, rows, width), BF16)
    out_shape = [full] * 2 if last else [one, half] * 2
    return pl.pallas_call(
        functools.partial(own_body, last, whole),
        in_specs=[scalars] * 3 + [near] * 2 + [far] * 4,
        out_specs=[far] * len(out_shape) + [near, scalars],
        out_shape=out_shape + [jax.ShapeDtypeStruct((matrices, rows, width), BF16), INFO],
        scratch_shapes=[
            pltpu.VMEM((2, matrices, rows, width), F32),
            pltpu.VMEM((2, matrices, rows, width), F32),
            pltpu.VMEM((matrices, rows, width), BF16),
            pltpu.VMEM((matrices, rows, width), BF16),
            pltpu.SemaphoreType.DMA((4, matrices)),
            pltpu.SemaphoreType.DMA((4, matrices)),
        ],
        compiler_params=params(),
        cost_estimate=cost(matrices * 6 * 2 * width**3, matrices * 16 * rows * width),
        name="own_update",
    )(info, rate, step, mine, theirs, *state)


def rest_body(slots, start, last, info, rate, step, *refs):
    gas, gbs = refs[:slots], refs[slots : 2 * slots]
    m_own, m_oth, w_own, w_oth = refs[2 * slots : 2 * slots + 4]
    count = 2 if last else 4
    outs = refs[-count - 3 : -3]
    info_out, g_own, g_oth = refs[-3:]
    hand_on(info, info_out)
    head = info[0] ^ (pl.program_id(0) + start)
    for slot in range(slots):

        @pl.when(pl.program_id(0) == slot)
        def _():
            g_own[...] = gas[slot][...]
            g_oth[...] = gbs[slot][...]

    def plan(j):
        def save(kind, own, oth):
            first = 0 if kind == "moment" else count // 2
            outs[first][0, j] = own
            if not last:
                outs[first + 1][0, j] = oth.astype(BF16)

        return stages(
            rate[head], step[head],
            (lambda: g_own[j].astype(F32), lambda: g_oth[j].astype(F32)),
            (lambda: m_own[0, j], lambda: m_oth[0, j].astype(F32)),
            (lambda: w_own[0, j], lambda: w_oth[0, j].astype(F32)),
            save,
        )

    interleave([plan(j) for j in range(m_own.shape[1])], REST_SKEW)


def rest_update(info, rate, step, gas, gbs, state, previous, start, last):
    heads, matrices, rows, width = state[0].shape
    slots = len(gas)
    block = pl.BlockSpec((1, matrices, rows, width), lambda s, info: (info[0] ^ (s + start), 0, 0, 0))
    scalars = pl.BlockSpec(memory_space=pltpu.SMEM)
    far = pl.BlockSpec(memory_space=pltpu.HBM)
    full = jax.ShapeDtypeStruct((heads, matrices, rows, width), F32)
    half = jax.ShapeDtypeStruct((heads, matrices, rows, width), BF16)
    out_shape = [full] * 2 if last else [full, half] * 2
    kept = list(previous or [])
    arrived = pl.BlockSpec((matrices, rows, width), lambda s, info: (0, 0, 0))
    return pl.pallas_call(
        functools.partial(rest_body, slots, start, last),
        grid_spec=pltpu.PrefetchScalarGridSpec(
            num_scalar_prefetch=1,
            grid=(slots,),
            in_specs=[scalars] * 2 + [arrived] * (2 * slots) + [block] * 4 + [far] * len(kept),
            out_specs=[block] * len(out_shape) + [scalars],
            scratch_shapes=[pltpu.VMEM((matrices, rows, width), BF16)] * 2,
        ),
        out_shape=out_shape + [INFO],
        input_output_aliases={7 + 2 * slots + i: i for i in range(len(kept))},
        compiler_params=params(),
        cost_estimate=cost(
            slots * matrices * 6 * 2 * width**3, slots * matrices * 16 * rows * width
        ),
        name="rest_update",
    )(info, rate, step, *gas, *gbs, *state, *kept)


def gate_body(info, *refs):
    hand_on(info, refs[-1])


def hold(info, awaited):
    scalars = pl.BlockSpec(memory_space=pltpu.SMEM)
    return pl.pallas_call(
        gate_body,
        in_specs=[scalars] + [pl.BlockSpec(memory_space=pl.ANY)] * len(awaited),
        out_specs=scalars,
        out_shape=INFO,
        compiler_params=params(),
        cost_estimate=cost(0, 0),
        name="hold",
    )(info, *awaited)


def gate(info, arrays):
    scalars = pl.BlockSpec(memory_space=pltpu.SMEM)
    far = pl.BlockSpec(memory_space=pl.ANY)
    *arrays, info = pl.pallas_call(
        gate_body,
        in_specs=[scalars] + [far] * len(arrays),
        out_specs=[far] * len(arrays) + [scalars],
        out_shape=[jax.ShapeDtypeStruct(value.shape, value.dtype) for value in arrays] + [INFO],
        input_output_aliases={1 + i: i for i in range(len(arrays))},
        compiler_params=params(),
        cost_estimate=cost(0, 0),
        name="gate",
    )(info, *arrays)
    return (*arrays, info)


def mix_body(block, kept, alone, info, queries, keys, values, *refs):
    early = refs[: 4 if block else 2]
    refs = refs[len(early) :]
    own, other, *lone = refs[: 2 + alone]
    out, info_out, weights = refs[2 + alone + kept :]
    hand_on(info, info_out)
    length, width = queries.shape[1:]

    def place_all(own, other):
        for matrix in range(own.shape[1]):
            place_halves(info, weights.at[matrix], own[0, matrix], other[0, matrix])

    if alone:
        pl.when(pl.program_id(0) == 0)(lambda: place_all(*lone))
        pl.when(pl.program_id(0) > 0)(lambda: place_all(own, other))
    else:
        place_all(own, other)
    query_unit = unit(queries[0])
    gate = dot(query_unit, weights[0])
    hidden = (gate * sigmoid(gate) * dot(query_unit, weights[1])).astype(BF16)
    recall = dot(hidden, weights[2])
    rows = lax.broadcasted_iota(jnp.int32, (length, length), 0)
    lanes = lax.broadcasted_iota(jnp.int32, (length, length), 1)
    here = lanes <= rows
    factor = HEAD_DIM ** (-0.5) * float(np.log2(np.e))
    for head in range(width // HEAD_DIM):
        columns = slice(head * HEAD_DIM, (head + 1) * HEAD_DIM)
        query = queries[0, :, columns]
        early_k, early_v = early[0][0, :, columns], early[1][0, :, columns]
        if block:
            early_k = jnp.where(info[2] == 1, early_k, early[2][0, :, columns])
            early_v = jnp.where(info[2] == 1, early_v, early[3][0, :, columns])
        scores = dot_nt(query, early_k)
        if block == 0:
            scores = scores + jnp.where(info[2] == 1, -1e30, 0.0)
        scores = jnp.where(here, dot_nt(query, keys[0, :, columns]), scores)
        top = jnp.max(scores, axis=1, keepdims=True)
        expo = jnp.exp2((scores - top) * factor)
        total = jnp.sum(expo, axis=1, keepdims=True)
        result = dot(jnp.where(here, expo, 0.0).astype(BF16), values[0, :, columns])
        result += dot(jnp.where(here, 0.0, expo).astype(BF16), early_v)
        out[0, :, columns] = (result * (1.0 / total) + recall[:, columns]).astype(BF16)


def mix(block, info, queries, keys, values, early, own, other, lone, previous):
    groups, length, width = queries.shape
    heads = own.shape[0]
    part = width // heads
    here = pl.BlockSpec((1, length, part), lambda s, info: (block, 0, info[0] ^ s))
    before = [
        pl.BlockSpec((1, length, part), lambda s, info: (0, 0, info[0] ^ s)),
        pl.BlockSpec((1, length, part), lambda s, info: (1, 0, info[0] ^ s)),
    ]
    early = [tail for tail in early for _ in range(2)]
    shape = (1,) + own.shape[1:]
    if lone:
        weight = pl.BlockSpec(shape, lambda s, info: (info[0] ^ jnp.maximum(s, 1), 0, 0, 0))
    else:
        weight = pl.BlockSpec(shape, lambda s, info: (info[0] ^ s, 0, 0, 0))
    kept = [] if previous is None else [previous]
    return pl.pallas_call(
        functools.partial(mix_body, block, len(kept), len(lone)),
        grid_spec=pltpu.PrefetchScalarGridSpec(
            num_scalar_prefetch=1,
            grid=(heads,),
            in_specs=[here] * 3 + before * (len(early) // 2) + [weight] * 2
            + [pl.BlockSpec(shape, lambda s, info: (0, 0, 0, 0))] * len(lone)
            + [pl.BlockSpec(memory_space=pltpu.HBM)] * len(kept),
            out_specs=[here, pl.BlockSpec(memory_space=pltpu.SMEM)],
            scratch_shapes=[pltpu.VMEM((3, part, part), BF16)],
        ),
        out_shape=[jax.ShapeDtypeStruct(queries.shape, BF16), INFO],
        input_output_aliases={6 + len(early) + len(lone): 0} if kept else {},
        compiler_params=params(),
        cost_estimate=cost(
            heads * (6 * length * part * part + 8 * length * length * part),
            12 * length * width + 12 * width * part,
        ),
        name="mix",
    )(info, queries, keys, values, *early, own, other, *lone, *kept)


def owner_shards(queries, keys, values, token_lr, momentum_rate, update_step, fast_weights, momentum):
    groups, length, _ = queries.shape
    chips = lax.axis_size("tok")
    chip = lax.axis_index("tok")
    row = lax.axis_index("row")
    first = (lax.axis_index(("tok", "row")) == 0).astype(jnp.int32)
    info = jnp.stack([chip, row, first]).astype(jnp.int32)
    rates = jnp.transpose(token_lr, (1, 2, 0))
    scalars = (momentum_rate, update_step)

    def to_chip(value, slot):
        return lax.ppermute(value, "tok", [(c, c ^ slot) for c in range(chips)])

    def to_core(value):
        return lax.ppermute(value, "row", [(0, 1), (1, 0)])

    def swap(pieces):
        return [to_core(piece) for piece in pieces]

    def pass_on(piece, wrap):
        places = chips * lax.axis_size("row")
        pairs = [(d, (d + 1) % places) for d in range(places - (not wrap))]
        return lax.ppermute(piece, ("tok", "row"), pairs)

    def spread(value):
        return [to_chip(value, slot) for slot in range(1, chips)]

    state = (momentum, to_core(momentum), fast_weights, to_core(fast_weights))
    *sent, first_tail, second_tail, info = prep(info, keys, values, rates)
    parts = [sent[0]] + [to_chip(sent[slot], slot) for slot in range(1, chips)]
    info = hold(info, [state[1], state[3]])
    early = [pass_on(first_tail, True)]
    partial, info = grad(0, info, parts, *state[2:])
    *lone, shared, info = own_update(info, *scalars, partial, to_core(partial), state, False)
    arrived = spread(shared)
    partial, info = grad(1, info, parts, *lone[2:])
    *chain, shared, info = own_update(info, *scalars, partial, to_core(partial), lone, True)
    arrived += spread(shared)
    mixed, info = mix(0, info, queries, keys, values, early, *state[2:], (), None)
    *gas, second_tail, info = gate(info, arrived[: chips - 1] + [second_tail])
    early.append(pass_on(second_tail, False))
    *state, info = rest_update(info, *scalars, gas, swap(gas), state, None, 1, False)
    for start, stop in ((1, chips - 1), (chips - 1, chips)):
        *gas, info = gate(info, arrived[chips - 2 + start : chips - 2 + stop])
        *chain, info = rest_update(info, *scalars, gas, swap(gas), state, chain, start, True)
    mixed, info = mix(1, info, queries, keys, values, early, *state[2:], lone[2:], mixed)
    moment, weights = chain
    return (mixed, weights, moment)


def shards(chips, queries, *rest):
    heads = queries.shape[2] // DH
    if heads == chips and chips & (chips - 1) == 0 and queries.shape[:2] == (2, WINDOW):
        return owner_shards(queries, *rest)
    return general_shards(queries, *rest)


def solution(mesh):
    return jax.shard_map(
        functools.partial(shards, mesh.shape["tok"]),
        mesh=mesh,
        in_specs=(
            P(None, ("tok", "row"), "mem"),
            P(None, ("tok", "row"), "mem"),
            P(None, ("tok", "row"), "mem"),
            P("mem", None, ("tok", "row")),
            P("mem"),
            P("mem"),
            P("mem", None, "row", None),
            P("mem", None, "row", None),
        ),
        out_specs=(
            P(None, ("tok", "row"), "mem"),
            P("mem", None, "row", None),
            P("mem", None, "row", None),
        ),
        check_vma=False,
    )
```

```python
import functools

import jax
import jax.numpy as jnp
import numpy as np
from jax import lax
from jax.experimental import pallas as pl
from jax.experimental.pallas import tpu as pltpu
from jax.sharding import PartitionSpec as P

DH = 512
HEAD_DIM = 128
WINDOW = 256
NS_STEPS = 2
GROUPS = 2


quintic_one = 3.4445
quintic_two = -4.775
quintic_three = 2.0315


def shifted(value, axis, steps):
    count = lax.axis_size(axis)
    pairs = [(source, (source + steps) % count) for source in range(count)]
    return lax.ppermute(value, axis, pairs)


def unit_rows(field):
    field = field.astype(jnp.float32)
    return field * lax.rsqrt(jnp.mean(field * field, axis=-1, keepdims=True) + 1e-05)


def refine(ortho, gram):
    gram_half = gram.astype(jnp.bfloat16)
    square = jnp.einsum("hmde,hmef->hmdf", gram_half, gram_half, preferred_element_type=jnp.float32)
    poly = (quintic_two * gram + quintic_three * square).astype(jnp.bfloat16)
    turned = jnp.einsum("hmrd,hmde->hmre", ortho, poly, preferred_element_type=jnp.float32)
    return (quintic_one * ortho.astype(jnp.float32) + turned).astype(jnp.bfloat16)


def sliding_attention(queries, keys, values):
    groups, local_len, local_width = queries.shape
    heads = local_width // HEAD_DIM
    tails = jnp.stack([keys, values], axis=0)
    received = shifted(tails, ("tok", "row"), 1)
    device = lax.axis_index(("tok", "row"))
    earlier = jnp.concatenate([jnp.zeros_like(received[:, :1]), received[:, :-1]], axis=1)
    halo = jnp.where(device == 0, earlier, received)
    ext_keys = jnp.concatenate([halo[0], keys], axis=1)
    ext_values = jnp.concatenate([halo[1], values], axis=1)
    block_len = min(local_len, 512)
    count = local_len // block_len
    group_total = local_len * lax.axis_size(("tok", "row"))
    scale = HEAD_DIM ** (-0.5)
    group_base = jnp.arange(groups, dtype=jnp.int32) * group_total + device * local_len

    def attend(block):
        start = block * block_len
        span = block_len + WINDOW
        query_part = queries.reshape(groups, block_len, heads, HEAD_DIM)
        key_part = ext_keys.reshape(groups, span, heads, HEAD_DIM)
        value_part = ext_values.reshape(groups, span, heads, HEAD_DIM)
        scores = (
            jnp.einsum("cqae,ckae->caqk", query_part, key_part, preferred_element_type=jnp.float32)
            * scale
        )
        query_local = start + jnp.arange(block_len, dtype=jnp.int32)
        key_local = start - WINDOW + jnp.arange(span, dtype=jnp.int32)
        offset = query_local[:, None] - key_local[None, :]
        near = (offset >= 0) & (offset < WINDOW)
        placed = group_base[:, None] + key_local[None, :] >= 0
        allowed = near[None, None, :, :] & placed[:, None, None, :]
        scores = jnp.where(allowed, scores, -1e30)
        top = jnp.max(scores, axis=-1, keepdims=True)
        expo = jnp.exp(scores - top)
        probs = (expo / jnp.sum(expo, axis=-1, keepdims=True)).astype(jnp.bfloat16)
        result = jnp.einsum(
            "caqk,ckae->cqae", probs, value_part, preferred_element_type=jnp.float32
        )
        return result.reshape(groups, block_len, local_width)

    pieces = lax.map(attend, jnp.arange(count, dtype=jnp.int32))
    return jnp.moveaxis(pieces, 0, 1).reshape(groups, local_len, local_width)


def general_shards(queries, keys, values, token_lr, momentum_rate, update_step, fast_weights, momentum):
    attended = sliding_attention(queries, keys, values)
    groups, local_len, local_width = queries.shape
    heads_local = local_width // DH
    query_unit = unit_rows(queries.reshape(groups, local_len, heads_local, DH)).astype(jnp.bfloat16)
    key_unit = unit_rows(keys.reshape(groups, local_len, heads_local, DH)).astype(jnp.bfloat16)
    value_heads = values.reshape(groups, local_len, heads_local, DH)
    rows = fast_weights.shape[2]
    row_start = lax.axis_index("row") * rows
    weights = fast_weights
    moment = momentum
    recalls = []
    for index in range(GROUPS):
        half = lax.all_gather(weights.astype(jnp.bfloat16), "row", axis=2, tiled=True)
        gate_w = half[:, 0]
        up_w = half[:, 1]
        down_w = half[:, 2]
        query_gate = jnp.einsum(
            "lhd,hdf->lhf", query_unit[index], gate_w, preferred_element_type=jnp.float32
        )
        query_up = jnp.einsum(
            "lhd,hdf->lhf", query_unit[index], up_w, preferred_element_type=jnp.float32
        )
        query_hidden = (jax.nn.silu(query_gate) * query_up).astype(jnp.bfloat16)
        recall = jnp.einsum(
            "lhf,hfd->lhd", query_hidden, down_w, preferred_element_type=jnp.float32
        )
        recalls.append(recall.reshape(local_len, local_width))
        key_gate = jnp.einsum(
            "lhd,hdf->lhf", key_unit[index], gate_w, preferred_element_type=jnp.float32
        )
        key_up = jnp.einsum(
            "lhd,hdf->lhf", key_unit[index], up_w, preferred_element_type=jnp.float32
        )
        key_hidden = (jax.nn.silu(key_gate) * key_up).astype(jnp.bfloat16)
        rate = jnp.transpose(token_lr[:, index, :])[:, :, None]
        target = (-(rate * value_heads[index].astype(jnp.float32))).astype(jnp.bfloat16)
        back = jnp.einsum("lhd,hfd->lhf", target, down_w, preferred_element_type=jnp.float32)
        sig = jax.nn.sigmoid(key_gate)
        gate_in = (back * key_up * sig * (1.0 + key_gate * (1.0 - sig))).astype(jnp.bfloat16)
        up_in = (back * jax.nn.silu(key_gate)).astype(jnp.bfloat16)
        gradient = jnp.stack(
            [
                jnp.einsum(
                    "lhd,lhf->hdf", key_unit[index], gate_in, preferred_element_type=jnp.float32
                ),
                jnp.einsum(
                    "lhd,lhf->hdf", key_unit[index], up_in, preferred_element_type=jnp.float32
                ),
                jnp.einsum("lhf,lhd->hfd", key_hidden, target, preferred_element_type=jnp.float32),
            ],
            axis=1,
        )
        halves = lax.psum_scatter(
            gradient.astype(jnp.bfloat16), "row", scatter_dimension=2, tiled=True
        )
        owned = lax.psum(halves, "tok").astype(jnp.float32)
        moment = momentum_rate[:, None, None, None] * moment + owned
        whole = lax.all_gather(moment.astype(jnp.bfloat16), "row", axis=2, tiled=True).astype(
            moment.dtype
        )
        ortho = (
            whole * lax.rsqrt(jnp.sum(whole * whole, axis=(2, 3), keepdims=True) + 1e-06)
        ).astype(jnp.bfloat16)
        for turn in range(NS_STEPS):
            gram = jnp.einsum("hmrd,hmre->hmde", ortho, ortho, preferred_element_type=jnp.float32)
            ortho = refine(ortho, gram)
        ortho = lax.dynamic_slice_in_dim(ortho, row_start, rows, 2)
        stepped = weights - update_step[:, None, None, None] * ortho.astype(jnp.float32)
        columns = lax.psum(jnp.sum(stepped * stepped, axis=2), "row")
        weights = stepped * lax.rsqrt(columns[:, :, None, :] + 1e-06)
    mixed = (attended + jnp.stack(recalls, axis=0)).astype(jnp.bfloat16)
    return (mixed, weights, moment)


F32 = jnp.float32
BF16 = jnp.bfloat16
SHARE = 0.05
VMEM_LIMIT = 48 * 1024 * 1024


def dot(a, b):
    return lax.dot_general(a, b, (((1,), (0,)), ((), ())), preferred_element_type=F32)


def dot_tn(a, b):
    return lax.dot_general(a, b, (((0,), (0,)), ((), ())), preferred_element_type=F32)


def dot_nt(a, b):
    return lax.dot_general(a, b, (((1,), (1,)), ((), ())), preferred_element_type=F32)


def unit(field):
    field = field.astype(F32)
    mean = jnp.mean(field * field, axis=-1, keepdims=True)
    return (field * lax.rsqrt(mean + 1e-05)).astype(BF16)


def sigmoid(value):
    return 1.0 / (1.0 + jnp.exp(-value))


def params(**more):
    return pltpu.CompilerParams(vmem_limit_bytes=VMEM_LIMIT, **more)


def cost(flops, moved):
    return pl.CostEstimate(flops=int(flops * SHARE), bytes_accessed=int(moved * SHARE), transcendentals=0)


TOKEN = jax.ShapeDtypeStruct((8, 128), jnp.float32)
PASSED = pl.BlockSpec(memory_space=pl.ANY)


def prep_body(groups, info, keys, values, rates, token, *refs):
    sends, tails = refs[: -groups - 1], refs[-groups - 1 : -1]

    for group, tail in enumerate(tails):

        @pl.when(pl.program_id(0) == group)
        def _():
            tail[0] = keys[0]
            tail[1] = values[0]

    rate_all = rates[0]
    lanes = lax.broadcasted_iota(jnp.int32, rate_all.shape, 1)
    width = sends[0].shape[-1]
    for slot, out in enumerate(sends):
        head = info[0] ^ slot
        columns = pl.ds(pl.multiple_of(head * width, width), width)
        out[0, 0] = unit(keys[0, :, columns])
        rate = jnp.sum(jnp.where(lanes == head, rate_all, 0.0), axis=1, keepdims=True)
        out[0, 1] = (-(rate * values[0, :, columns].astype(F32))).astype(BF16)


def prep(chain, keys, values, rates):
    info, token = chain
    groups, length, width = keys.shape
    heads = rates.shape[-1]
    part = width // heads
    return pl.pallas_call(
        functools.partial(prep_body, groups),
        grid_spec=pltpu.PrefetchScalarGridSpec(
            num_scalar_prefetch=1,
            grid=(groups,),
            in_specs=[
                pl.BlockSpec((1, length, width), lambda i, info: (i, 0, 0)),
                pl.BlockSpec((1, length, width), lambda i, info: (i, 0, 0)),
                pl.BlockSpec((1, length, heads), lambda i, info: (i, 0, 0)),
                PASSED,
            ],
            out_specs=[pl.BlockSpec((1, 2, length, part), lambda i, info: (i, 0, 0, 0))] * heads
            + [pl.BlockSpec((2, length, width), lambda i, info: (0, 0, 0))] * groups
            + [PASSED],
        ),
        out_shape=[jax.ShapeDtypeStruct((groups, 2, length, part), BF16)] * heads
        + [jax.ShapeDtypeStruct((2, length, width), BF16)] * groups
        + [TOKEN],
        input_output_aliases={4: heads + groups},
        compiler_params=params(),
        cost_estimate=cost(0, 12 * groups * length * width),
        name="prep",
    )(info, keys, values, rates, token)


def place_halves(info, target, own, other):
    rows = own.shape[0]
    target[pl.ds(pl.multiple_of(info[1] * rows, rows), rows), :] = own.astype(BF16)
    target[pl.ds(pl.multiple_of((1 - info[1]) * rows, rows), rows), :] = other.astype(BF16)


def grad_body(block, slots, info, *refs):
    parts = refs[:slots]
    own, other, token, out, token_out, weights, units, targets, hidden, gates, ups = refs[slots:]
    length = parts[0].shape[2]
    own, other = (ref if len(ref.shape) == 3 else ref.at[0] for ref in (own, other))
    for matrix in range(3):
        place_halves(info, weights.at[matrix], own[matrix], other[matrix])
    for slot, part in enumerate(parts):
        span = pl.ds(slot * length, length)
        key_unit = part[block, 0]
        target = part[block, 1]
        units[span, :] = key_unit
        targets[span, :] = target
        key_gate = dot(key_unit, weights[0])
        key_up = dot(key_unit, weights[1])
        back = dot_nt(target, weights[2])
        sig = sigmoid(key_gate)
        silu = key_gate * sig
        hidden[span, :] = (silu * key_up).astype(BF16)
        gates[span, :] = (back * key_up * sig * (1.0 + key_gate * (1.0 - sig))).astype(BF16)
        ups[span, :] = (back * silu).astype(BF16)
    rows = own.shape[1]
    for half in range(2):
        place = info[1] if half == 0 else 1 - info[1]
        columns = pl.ds(pl.multiple_of(place * rows, rows), rows)
        out[half, 0] = dot_tn(units[:, columns], gates[...]).astype(BF16)
        out[half, 1] = dot_tn(units[:, columns], ups[...]).astype(BF16)
        out[half, 2] = dot_tn(hidden[:, columns], targets[...]).astype(BF16)


def head_spec(shape):
    if len(shape) == 3:
        return pl.BlockSpec(memory_space=pltpu.VMEM)
    return pl.BlockSpec((1,) + shape[1:], lambda i, info: (info[0], 0, 0, 0))


def grad(block, chain, parts, own, other):
    info, token = chain
    slots = len(parts)
    _, _, length, width = parts[0].shape
    rows = own.shape[-2]
    total = slots * length
    return pl.pallas_call(
        functools.partial(grad_body, block, slots),
        grid_spec=pltpu.PrefetchScalarGridSpec(
            num_scalar_prefetch=1,
            grid=(1,),
            in_specs=[pl.BlockSpec(memory_space=pltpu.VMEM)] * slots
            + [head_spec(own.shape)] * 2
            + [PASSED],
            out_specs=[
                pl.BlockSpec((2, 3, rows, width), lambda i, info: (0, 0, 0, 0)),
                PASSED,
            ],
            scratch_shapes=[pltpu.VMEM((3, width, width), BF16)]
            + [pltpu.VMEM((total, width), BF16)] * 5,
        ),
        out_shape=[jax.ShapeDtypeStruct((2, 3, rows, width), BF16), TOKEN],
        input_output_aliases={3 + slots: 1},
        compiler_params=params(),
        cost_estimate=cost(12 * total * width * width, 4 * total * width + 15 * width * width),
        name="grad",
    )(info, *parts, own, other, token)


OWN_SKEW = 0
REST_SKEW = 0
CHUNK = 32


def fold(value):
    return jnp.sum(value.reshape(-1, 8, value.shape[-1]), axis=0)


def stages(rate, step, begun, gradient, moment, weight, put, x):
    rows = x.shape[0] // 2
    chunks = [(half, pl.ds(at, CHUNK)) for half in range(2) for at in range(0, rows, CHUNK)]
    held = {}

    def after(half, part):
        return rate * moment(half, part) + gradient(half, part)

    def stepped(half, part):
        return weight(half, part) - step * x[pl.ds(half * rows + part.start, CHUNK)].astype(F32)

    def begin():
        begun("moment")
        total = 0.0
        for half, part in chunks:
            value = after(half, part)
            total += fold(value * value)
        scale = lax.rsqrt(jnp.sum(total, keepdims=True) + 1e-06)
        for half, part in chunks:
            value = after(half, part)
            x[pl.ds(half * rows + part.start, CHUNK)] = (value * scale).astype(BF16)
            put("moment", half, part, value)
        put("moment", None, None, None)

    def gram():
        held["gram"] = dot_tn(x[...], x[...])

    def poly():
        half = held["gram"].astype(BF16)
        held["poly"] = (quintic_two * held["gram"] + quintic_three * dot(half, half)).astype(BF16)

    def turn():
        turned = quintic_one * x[...].astype(F32) + dot(x[...], held["poly"])
        x[...] = turned.astype(BF16)

    def finish():
        begun("weight")
        total = 0.0
        for half, part in chunks:
            value = stepped(half, part)
            total += fold(value * value)
        scale = lax.rsqrt(jnp.sum(total, axis=0, keepdims=True) + 1e-06)
        for half, part in chunks:
            put("weight", half, part, stepped(half, part) * scale)
        put("weight", None, None, None)

    return [begin] + [gram, poly, turn] * NS_STEPS + [finish]


def interleave(work, skew):
    for now in range(len(work[0]) + skew * (len(work) - 1)):
        for place, steps in enumerate(work):
            if 0 <= now - skew * place < len(steps):
                steps[now - skew * place]()


def own_body(info, rate, step, mine, theirs, *refs):
    state, (w_own, w_oth, token_out, moments, weights, x, load_sem) = refs[:4], refs[5:]
    head = info[0]
    matrices = w_own.shape[0]
    homes = [moments.at[0], moments.at[1], weights.at[0], weights.at[1]]
    loads = [
        [
            pltpu.make_async_copy(value.at[head, j], home.at[j], load_sem.at[i, j])
            for j in range(matrices)
        ]
        for i, (value, home) in enumerate(zip(state, homes))
    ]
    for group in loads:
        for load in group:
            load.start()

    def plan(j):
        def begun(kind):
            for i in (0, 1) if kind == "moment" else (2, 3):
                loads[i][j].wait()

        def put(kind, half, part, value):
            if kind == "weight" and half is not None:
                (w_own, w_oth)[half][j, part] = value.astype(BF16)

        return stages(
            rate[head], step[head], begun,
            lambda half, part: mine[half, j, part].astype(F32) + theirs[1 - half, j, part].astype(F32),
            lambda half, part: moments[half, j, part],
            lambda half, part: weights[half, j, part],
            put, x.at[j],
        )

    interleave([plan(j) for j in range(matrices)], OWN_SKEW)


def own_update(chain, rate, step, mine, theirs, state):
    info, token = chain
    _, matrices, rows, width = state[0].shape
    scalars = pl.BlockSpec(memory_space=pltpu.SMEM)
    near = pl.BlockSpec(memory_space=pltpu.VMEM)
    far = pl.BlockSpec(memory_space=pltpu.HBM)
    half = jax.ShapeDtypeStruct((matrices, rows, width), BF16)
    return pl.pallas_call(
        own_body,
        in_specs=[scalars] * 3 + [near] * 2 + [far] * 4 + [PASSED],
        out_specs=[near] * 2 + [PASSED],
        out_shape=[half, half, TOKEN],
        input_output_aliases={9: 2},
        scratch_shapes=[
            pltpu.VMEM((2, matrices, rows, width), F32),
            pltpu.VMEM((2, matrices, rows, width), F32),
            pltpu.VMEM((matrices, 2 * rows, width), BF16),
            pltpu.SemaphoreType.DMA((4, matrices)),
        ],
        compiler_params=params(),
        cost_estimate=cost(matrices * 6 * 2 * width**3, matrices * 16 * rows * width),
        name="own_update",
    )(info, rate, step, mine, theirs, *state, token)


def total_body(info, rate, first, first_other, second, second_other, token, own, oth, token_out):
    for half, out in enumerate((own, oth)):
        for matrix in range(out.shape[0]):
            for at in range(0, out.shape[1], CHUNK):
                part = pl.ds(at, CHUNK)
                early = first[half, matrix, part].astype(F32)
                early += first_other[1 - half, matrix, part].astype(F32)
                late = second[half, matrix, part].astype(F32)
                late += second_other[1 - half, matrix, part].astype(F32)
                out[matrix, part] = (rate[info[0]] * early + late).astype(BF16)


def total_gradient(chain, rate, pieces):
    info, token = chain
    _, matrices, rows, width = pieces[0].shape
    scalars = pl.BlockSpec(memory_space=pltpu.SMEM)
    near = pl.BlockSpec(memory_space=pltpu.VMEM)
    half = jax.ShapeDtypeStruct((matrices, rows, width), BF16)
    return pl.pallas_call(
        total_body,
        in_specs=[scalars] * 2 + [near] * 4 + [PASSED],
        out_specs=[near] * 2 + [PASSED],
        out_shape=[half, half, TOKEN],
        input_output_aliases={6: 2},
        compiler_params=params(),
        cost_estimate=cost(0, 20 * matrices * rows * width),
        name="total_gradient",
    )(info, rate, *pieces, token)


def last_body(slots, start, places, info, rate, step, *refs):
    ready, refs = refs[: 4 * slots], refs[4 * slots :]
    m_own, m_oth = refs[:2]
    m_out, w_out, token_out, held, x = refs[-5:]
    head = info[0] ^ (pl.program_id(0) + start)
    for slot in range(slots):

        @pl.when(pl.program_id(0) == slot)
        def _():
            for i in range(4):
                held[i] = pick(ready[4 * slot + i], places[4 * slot + i])[...]

    def plan(j):
        def put(kind, half, part, value):
            if half == 0:
                (m_out if kind == "moment" else w_out)[0, j, part] = value

        return stages(
            rate[head] * rate[head], step[head], lambda kind: None,
            lambda half, part: held[half, j, part].astype(F32),
            lambda half, part: (m_own, m_oth)[half][0, j, part],
            lambda half, part: held[2 + half, j, part].astype(F32),
            put, x.at[j],
        )

    interleave([plan(j) for j in range(m_own.shape[1])], REST_SKEW)


def last_update(chain, rate, step, gradients, weights, state, previous, start):
    info, token = chain
    heads, matrices, rows, width = state[0].shape
    slots = len(gradients)
    block = pl.BlockSpec((1, matrices, rows, width), lambda s, info: (info[0] ^ (s + start), 0, 0, 0))
    scalars = pl.BlockSpec(memory_space=pltpu.SMEM)
    near = pl.BlockSpec(memory_space=pltpu.VMEM)
    far = pl.BlockSpec(memory_space=pltpu.HBM)
    full = jax.ShapeDtypeStruct((heads, matrices, rows, width), F32)
    kept = list(previous or [])
    ready = [value for pair in zip(gradients, weights) for both in pair for value in both]
    places = [at for _, at in ready]
    ready = [value for value, _ in ready]
    return pl.pallas_call(
        functools.partial(last_body, slots, start, places),
        grid_spec=pltpu.PrefetchScalarGridSpec(
            num_scalar_prefetch=1,
            grid=(slots,),
            in_specs=[scalars] * 2 + [near] * (4 * slots) + [block] * 2 + [far] * len(kept)
            + [PASSED],
            out_specs=[block] * 2 + [PASSED],
            scratch_shapes=[
                pltpu.VMEM((4, matrices, rows, width), BF16),
                pltpu.VMEM((matrices, 2 * rows, width), BF16),
            ],
        ),
        out_shape=[full] * 2 + [TOKEN],
        input_output_aliases={5 + 4 * slots + i: i for i in range(len(kept))}
        | {5 + 4 * slots + len(kept): 2},
        compiler_params=params(),
        cost_estimate=cost(
            slots * matrices * 6 * 2 * width**3, slots * matrices * 16 * rows * width
        ),
        name="last_update",
    )(info, rate, step, *ready, *state, *kept, token)


def gate_body(*refs):
    pass


def gate(token, values):
    count = len(values) + 1
    return pl.pallas_call(
        gate_body,
        in_specs=[PASSED] * count,
        out_specs=[PASSED] * count,
        out_shape=[jax.ShapeDtypeStruct(value.shape, value.dtype) for value in values] + [TOKEN],
        input_output_aliases={i: i for i in range(count)},
        compiler_params=params(),
        cost_estimate=cost(0, 0),
        name="gate",
    )(*values, token)


def relay_body(x, y, token, both, to_x, to_y, token_out):
    rows = to_x.shape[1]
    both[0] = x[...]
    both[1] = y[...]
    to_x[...] = y[:, :rows]
    to_y[...] = x[:, rows:]


def relay(token, x, y):
    matrices, rows, width = x.shape
    near = pl.BlockSpec(memory_space=pltpu.VMEM)
    part = jax.ShapeDtypeStruct((matrices, rows // 2, width), x.dtype)
    return pl.pallas_call(
        relay_body,
        in_specs=[near] * 2 + [PASSED],
        out_specs=[near] * 3 + [PASSED],
        out_shape=[jax.ShapeDtypeStruct((2,) + x.shape, x.dtype), part, part, TOKEN],
        input_output_aliases={2: 3},
        compiler_params=params(),
        cost_estimate=cost(0, 6 * x.size),
        name="relay",
    )(x, y, token)


def join_body(from_x, from_y, token, out, token_out):
    rows = from_x.shape[1]
    out[:, :rows] = from_x[...]
    out[:, rows:] = from_y[...]


def join(token, from_x, from_y):
    matrices, rows, width = from_x.shape
    near = pl.BlockSpec(memory_space=pltpu.VMEM)
    return pl.pallas_call(
        join_body,
        in_specs=[near] * 2 + [PASSED],
        out_specs=[near, PASSED],
        out_shape=[jax.ShapeDtypeStruct((matrices, 2 * rows, width), from_x.dtype), TOKEN],
        input_output_aliases={2: 1},
        compiler_params=params(),
        cost_estimate=cost(0, 8 * from_x.size),
        name="join",
    )(from_x, from_y, token)


def pick(ref, at):
    return ref if at is None else ref.at[at]


def place_all(info, weights, halves, step):
    if len(halves[0][0].shape) == 4 and halves[0][1] is None:
        for matrix in range(weights.shape[0]):
            own, other = (ref[0, matrix] for ref, _ in halves)
            place_halves(info, weights.at[matrix], own, other)
        return
    for slot in range(len(halves) // 2):

        @pl.when(step == slot)
        def _():
            own, other = (pick(ref, at) for ref, at in halves[2 * slot : 2 * slot + 2])
            for matrix in range(weights.shape[0]):
                place_halves(info, weights.at[matrix], own[matrix], other[matrix])


def recall(query_unit, weights):
    gate = dot(query_unit, weights[0])
    hidden = (gate * sigmoid(gate) * dot(query_unit, weights[1])).astype(BF16)
    return dot(hidden, weights[2])


def attend(block, info, query, key, value, early_keys, early_values):
    length, width = query.shape
    rows = lax.broadcasted_iota(jnp.int32, (length, length), 0)
    lanes = lax.broadcasted_iota(jnp.int32, (length, length), 1)
    here = lanes <= rows
    early_key, early_value = early_keys[0], early_values[0]
    if block:
        early_key = jnp.where(info[2] == 1, early_key, early_keys[1])
        early_value = jnp.where(info[2] == 1, early_value, early_values[1])
    scores = dot_nt(query, early_key)
    if block == 0:
        scores = scores + jnp.where(info[2] == 1, -1e30, 0.0)
    scores = jnp.where(here, dot_nt(query, key), scores)
    top = jnp.max(scores, axis=1, keepdims=True)
    expo = jnp.exp2((scores - top) * (width ** (-0.5) * float(np.log2(np.e))))
    total = jnp.sum(expo, axis=1, keepdims=True)
    result = dot(jnp.where(here, expo, 0.0).astype(BF16), value)
    result += dot(jnp.where(here, 0.0, expo).astype(BF16), early_value)
    return result * (1.0 / total)


def mix_body(block, attends, places, info, queries, *refs):
    held = len(places)
    if attends:
        keys, values, *refs = refs
        early, refs = refs[: 2 + 2 * block], refs[2 + 2 * block :]
    else:
        attended, *refs = refs
    halves, refs = refs[:held], refs[held:]
    kept = len(refs) - 2 - (held > 0)
    out, token_out, *weights = refs[kept:]
    recalled = None
    if held:
        place_all(info, weights[0], list(zip(halves, places)), pl.program_id(0))
        recalled = recall(unit(queries[0]), weights[0])
    if not attends:
        out[0] = (attended[0] + recalled).astype(out.dtype)
        return
    for head in range(queries.shape[2] // HEAD_DIM):
        columns = slice(head * HEAD_DIM, (head + 1) * HEAD_DIM)
        result = attend(
            block, info, queries[0, :, columns], keys[0, :, columns], values[0, :, columns],
            [value[0, :, columns] for value in early[::2]],
            [value[0, :, columns] for value in early[1::2]],
        )
        if held:
            result = result + recalled[:, columns]
        out[0, :, columns] = result.astype(out.dtype)


def mix(block, chain, queries, heads, attention, halves, attended=None, previous=None, slots=None):
    info, token = chain
    groups, length, width = queries.shape
    part = width // heads
    start, stop = slots or (0, heads)

    def columns(at):
        return pl.BlockSpec((1, length, part), lambda s, info: (at, 0, info[0] ^ (s + start)))

    values, specs = [queries], [columns(block)]
    if attention:
        keys_values, early = attention
        values += keys_values + [value for value, _ in early]
        specs += [columns(block)] * 2 + [columns(at) for _, at in early]
    else:
        values.append(attended)
        specs.append(columns(0))
    places = [at for _, at in halves]
    halves = [value for value, _ in halves]
    values += halves
    if halves and halves[0].ndim == 4 and places[0] is None:
        shape = (1,) + halves[0].shape[1:]
        specs += [pl.BlockSpec(shape, lambda s, info: (info[0] ^ s, 0, 0, 0))] * 2
    else:
        specs += [pl.BlockSpec(memory_space=pltpu.VMEM)] * len(halves)
    aliases = {}
    if previous is not None:
        aliases = {1 + len(values): 0}
        values.append(previous)
        specs.append(pl.BlockSpec(memory_space=pltpu.HBM))
    aliases[1 + len(values)] = 1
    values.append(token)
    specs.append(PASSED)
    if halves:
        out, place = jax.ShapeDtypeStruct(queries.shape, BF16), block
    else:
        out, place = jax.ShapeDtypeStruct((1, length, width), F32), 0
    return pl.pallas_call(
        functools.partial(mix_body, block, attention is not None, places),
        grid_spec=pltpu.PrefetchScalarGridSpec(
            num_scalar_prefetch=1,
            grid=(stop - start,),
            in_specs=specs,
            out_specs=[columns(place), PASSED],
            scratch_shapes=[pltpu.VMEM((3, part, part), BF16)] if halves else [],
        ),
        out_shape=[out, TOKEN],
        input_output_aliases=aliases,
        compiler_params=params(),
        cost_estimate=cost((attention is not None) * 4e11, 0),
        name="mix",
    )(info, *values)


def owner_shards(queries, keys, values, token_lr, momentum_rate, update_step, fast_weights, momentum):
    groups, length, _ = queries.shape
    chips = lax.axis_size("tok")
    chip = lax.axis_index("tok")
    row = lax.axis_index("row")
    first = (lax.axis_index(("tok", "row")) == 0).astype(jnp.int32)
    info = jnp.stack([chip, row, first]).astype(jnp.int32)
    rates = jnp.transpose(token_lr, (1, 2, 0))
    scalars = (momentum_rate, update_step)

    def to_chip(value, slot):
        return lax.ppermute(value, "tok", [(c, c ^ slot) for c in range(chips)])

    def to_core(value):
        return lax.ppermute(value, "row", [(0, 1), (1, 0)])

    def pass_on(piece, wrap):
        places = chips * lax.axis_size("row")
        pairs = [(d, (d + 1) % places) for d in range(places - (not wrap))]
        return lax.ppermute(piece, ("tok", "row"), pairs)

    state = (momentum, to_core(momentum), fast_weights, to_core(fast_weights))
    token = jnp.zeros(TOKEN.shape, TOKEN.dtype)
    *sent, tail, last_tail, token = prep((info, token), keys, values, rates)
    parts = [sent[0]] + [to_chip(sent[slot], slot) for slot in range(1, chips)]
    first, token = grad(0, (info, token), parts, *state[2:])
    tail, last_tail, token = gate(token, [tail, last_tail])
    tails = [pass_on(tail, True), pass_on(last_tail, False)]
    pair = [keys, values]
    early = [(tail, at) for tail in tails for at in range(2)]
    pieces = [first, to_core(first)]
    w_own, w_oth, token = own_update((info, token), *scalars, *pieces, state)
    w_x, w_y = (to_chip(w_own, slot) for slot in (1, 2))
    second, token = grad(1, (info, token), parts, w_own, w_oth)
    halves = [(value, None) for value in state[2:]]
    mixed, token = mix(0, (info, token), queries, chips, (pair, early[:2]), halves)
    pieces += [second, to_core(second)]
    g_own, g_oth, token = total_gradient((info, token), momentum_rate, pieces)
    g_x, g_y = (to_chip(g_own, slot) for slot in (1, 2))

    def both_halves(value):
        return value, to_core(value)

    def each(halves, at=None):
        return [(half, at) for half in halves]

    def across(token, x, y):
        near, to_x, to_y, token = relay(token, x, y)
        near = both_halves(near)
        return [each(near, 0), each(near, 1)], (to_chip(to_x, 1), to_chip(to_y, 2)), token

    def last(token, gradients, weights, done, start):
        return last_update((info, token), *scalars, gradients, weights, state[:2], done, start)

    def recalls(token, mixed, weights, slots):
        halves = [value for both in weights for value in both]
        return mix(1, (info, token), queries, chips, None, halves, attended, mixed, slots)

    w_all = [each(both_halves(w_own))]
    *done, token = last(token, [each((g_own, g_oth))], w_all, None, 0)
    w_near, w_far, token = across(token, w_x, w_y)
    attended, token = mix(1, (info, token), queries, chips, (pair, early), [])
    mixed, token = recalls(token, mixed, w_all + w_near, (0, 3))
    g_near, g_far, token = across(token, g_x, g_y)
    *done, token = last(token, g_near, w_near, done, 1)
    w_far, token = join(token, *w_far)
    g_far, token = join(token, *g_far)
    w_far, g_far = (each(both_halves(value)) for value in (w_far, g_far))
    mixed, token = recalls(token, mixed, [w_far], (3, 4))
    moment, weights, token = last(token, [g_far], [w_far], done, 3)
    return (mixed, weights, moment)


def shards(chips, queries, *rest):
    heads = queries.shape[2] // DH
    if heads == chips == 4 and queries.shape[:2] == (GROUPS, WINDOW):
        return owner_shards(queries, *rest)
    return general_shards(queries, *rest)


def solution(mesh):
    return jax.shard_map(
        functools.partial(shards, mesh.shape["tok"]),
        mesh=mesh,
        in_specs=(
            P(None, ("tok", "row"), "mem"),
            P(None, ("tok", "row"), "mem"),
            P(None, ("tok", "row"), "mem"),
            P("mem", None, ("tok", "row")),
            P("mem"),
            P("mem"),
            P("mem", None, "row", None),
            P("mem", None, "row", None),
        ),
        out_specs=(
            P(None, ("tok", "row"), "mem"),
            P("mem", None, "row", None),
            P("mem", None, "row", None),
        ),
        check_vma=False,
    )
```

```python
import functools

import jax
import jax.numpy as jnp
import numpy as np
from jax import lax
from jax.experimental import pallas as pl
from jax.experimental.pallas import tpu as pltpu
from jax.sharding import PartitionSpec as P

DH = 512
HEAD_DIM = 128
WINDOW = 256
NS_STEPS = 2
GROUPS = 2


quintic_one = 3.4445
quintic_two = -4.775
quintic_three = 2.0315


def shifted(value, axis, steps):
    count = lax.axis_size(axis)
    pairs = [(source, (source + steps) % count) for source in range(count)]
    return lax.ppermute(value, axis, pairs)


def unit_rows(field):
    field = field.astype(jnp.float32)
    return field * lax.rsqrt(jnp.mean(field * field, axis=-1, keepdims=True) + 1e-05)


def refine(ortho, gram):
    gram_half = gram.astype(jnp.bfloat16)
    square = jnp.einsum("hmde,hmef->hmdf", gram_half, gram_half, preferred_element_type=jnp.float32)
    poly = (quintic_two * gram + quintic_three * square).astype(jnp.bfloat16)
    turned = jnp.einsum("hmrd,hmde->hmre", ortho, poly, preferred_element_type=jnp.float32)
    return (quintic_one * ortho.astype(jnp.float32) + turned).astype(jnp.bfloat16)


def sliding_attention(queries, keys, values):
    groups, local_len, local_width = queries.shape
    heads = local_width // HEAD_DIM
    tails = jnp.stack([keys, values], axis=0)
    received = shifted(tails, ("tok", "row"), 1)
    device = lax.axis_index(("tok", "row"))
    earlier = jnp.concatenate([jnp.zeros_like(received[:, :1]), received[:, :-1]], axis=1)
    halo = jnp.where(device == 0, earlier, received)
    ext_keys = jnp.concatenate([halo[0], keys], axis=1)
    ext_values = jnp.concatenate([halo[1], values], axis=1)
    block_len = min(local_len, 512)
    count = local_len // block_len
    group_total = local_len * lax.axis_size(("tok", "row"))
    scale = HEAD_DIM ** (-0.5)
    group_base = jnp.arange(groups, dtype=jnp.int32) * group_total + device * local_len

    def attend(block):
        start = block * block_len
        span = block_len + WINDOW
        query_part = queries.reshape(groups, block_len, heads, HEAD_DIM)
        key_part = ext_keys.reshape(groups, span, heads, HEAD_DIM)
        value_part = ext_values.reshape(groups, span, heads, HEAD_DIM)
        scores = (
            jnp.einsum("cqae,ckae->caqk", query_part, key_part, preferred_element_type=jnp.float32)
            * scale
        )
        query_local = start + jnp.arange(block_len, dtype=jnp.int32)
        key_local = start - WINDOW + jnp.arange(span, dtype=jnp.int32)
        offset = query_local[:, None] - key_local[None, :]
        near = (offset >= 0) & (offset < WINDOW)
        placed = group_base[:, None] + key_local[None, :] >= 0
        allowed = near[None, None, :, :] & placed[:, None, None, :]
        scores = jnp.where(allowed, scores, -1e30)
        top = jnp.max(scores, axis=-1, keepdims=True)
        expo = jnp.exp(scores - top)
        probs = (expo / jnp.sum(expo, axis=-1, keepdims=True)).astype(jnp.bfloat16)
        result = jnp.einsum(
            "caqk,ckae->cqae", probs, value_part, preferred_element_type=jnp.float32
        )
        return result.reshape(groups, block_len, local_width)

    pieces = lax.map(attend, jnp.arange(count, dtype=jnp.int32))
    return jnp.moveaxis(pieces, 0, 1).reshape(groups, local_len, local_width)


def general_shards(queries, keys, values, token_lr, momentum_rate, update_step, fast_weights, momentum):
    attended = sliding_attention(queries, keys, values)
    groups, local_len, local_width = queries.shape
    heads_local = local_width // DH
    query_unit = unit_rows(queries.reshape(groups, local_len, heads_local, DH)).astype(jnp.bfloat16)
    key_unit = unit_rows(keys.reshape(groups, local_len, heads_local, DH)).astype(jnp.bfloat16)
    value_heads = values.reshape(groups, local_len, heads_local, DH)
    rows = fast_weights.shape[2]
    row_start = lax.axis_index("row") * rows
    weights = fast_weights
    moment = momentum
    recalls = []
    for index in range(GROUPS):
        half = lax.all_gather(weights.astype(jnp.bfloat16), "row", axis=2, tiled=True)
        gate_w = half[:, 0]
        up_w = half[:, 1]
        down_w = half[:, 2]
        query_gate = jnp.einsum(
            "lhd,hdf->lhf", query_unit[index], gate_w, preferred_element_type=jnp.float32
        )
        query_up = jnp.einsum(
            "lhd,hdf->lhf", query_unit[index], up_w, preferred_element_type=jnp.float32
        )
        query_hidden = (jax.nn.silu(query_gate) * query_up).astype(jnp.bfloat16)
        recall = jnp.einsum(
            "lhf,hfd->lhd", query_hidden, down_w, preferred_element_type=jnp.float32
        )
        recalls.append(recall.reshape(local_len, local_width))
        key_gate = jnp.einsum(
            "lhd,hdf->lhf", key_unit[index], gate_w, preferred_element_type=jnp.float32
        )
        key_up = jnp.einsum(
            "lhd,hdf->lhf", key_unit[index], up_w, preferred_element_type=jnp.float32
        )
        key_hidden = (jax.nn.silu(key_gate) * key_up).astype(jnp.bfloat16)
        rate = jnp.transpose(token_lr[:, index, :])[:, :, None]
        target = (-(rate * value_heads[index].astype(jnp.float32))).astype(jnp.bfloat16)
        back = jnp.einsum("lhd,hfd->lhf", target, down_w, preferred_element_type=jnp.float32)
        sig = jax.nn.sigmoid(key_gate)
        gate_in = (back * key_up * sig * (1.0 + key_gate * (1.0 - sig))).astype(jnp.bfloat16)
        up_in = (back * jax.nn.silu(key_gate)).astype(jnp.bfloat16)
        gradient = jnp.stack(
            [
                jnp.einsum(
                    "lhd,lhf->hdf", key_unit[index], gate_in, preferred_element_type=jnp.float32
                ),
                jnp.einsum(
                    "lhd,lhf->hdf", key_unit[index], up_in, preferred_element_type=jnp.float32
                ),
                jnp.einsum("lhf,lhd->hfd", key_hidden, target, preferred_element_type=jnp.float32),
            ],
            axis=1,
        )
        halves = lax.psum_scatter(
            gradient.astype(jnp.bfloat16), "row", scatter_dimension=2, tiled=True
        )
        owned = lax.psum(halves, "tok").astype(jnp.float32)
        moment = momentum_rate[:, None, None, None] * moment + owned
        whole = lax.all_gather(moment.astype(jnp.bfloat16), "row", axis=2, tiled=True).astype(
            moment.dtype
        )
        ortho = (
            whole * lax.rsqrt(jnp.sum(whole * whole, axis=(2, 3), keepdims=True) + 1e-06)
        ).astype(jnp.bfloat16)
        for turn in range(NS_STEPS):
            gram = jnp.einsum("hmrd,hmre->hmde", ortho, ortho, preferred_element_type=jnp.float32)
            ortho = refine(ortho, gram)
        ortho = lax.dynamic_slice_in_dim(ortho, row_start, rows, 2)
        stepped = weights - update_step[:, None, None, None] * ortho.astype(jnp.float32)
        columns = lax.psum(jnp.sum(stepped * stepped, axis=2), "row")
        weights = stepped * lax.rsqrt(columns[:, :, None, :] + 1e-06)
    mixed = (attended + jnp.stack(recalls, axis=0)).astype(jnp.bfloat16)
    return (mixed, weights, moment)


F32 = jnp.float32
BF16 = jnp.bfloat16
SHARE = 0.05
VMEM_LIMIT = 48 * 1024 * 1024


def dot(a, b):
    return lax.dot_general(a, b, (((1,), (0,)), ((), ())), preferred_element_type=F32)


def dot_tn(a, b):
    return lax.dot_general(a, b, (((0,), (0,)), ((), ())), preferred_element_type=F32)


def dot_nt(a, b):
    return lax.dot_general(a, b, (((1,), (1,)), ((), ())), preferred_element_type=F32)


def unit(field):
    field = field.astype(F32)
    mean = jnp.mean(field * field, axis=-1, keepdims=True)
    return (field * lax.rsqrt(mean + 1e-05)).astype(BF16)


def sigmoid(value):
    return 1.0 / (1.0 + jnp.exp(-value))


def params(**more):
    return pltpu.CompilerParams(vmem_limit_bytes=VMEM_LIMIT, **more)


def cost(flops, moved):
    return pl.CostEstimate(flops=int(flops * SHARE), bytes_accessed=int(moved * SHARE), transcendentals=0)


TOKEN = jax.ShapeDtypeStruct((8, 128), jnp.float32)
PASSED = pl.BlockSpec(memory_space=pl.ANY)


def prep_body(info, keys, values, rates, token, *refs):
    sends = refs[:-1]

    rate_all = rates[0]
    lanes = lax.broadcasted_iota(jnp.int32, rate_all.shape, 1)
    width = sends[0].shape[-1]
    for slot, out in enumerate(sends):
        head = info[0] ^ slot
        columns = pl.ds(pl.multiple_of(head * width, width), width)
        out[0, 0] = unit(keys[0, :, columns])
        rate = jnp.sum(jnp.where(lanes == head, rate_all, 0.0), axis=1, keepdims=True)
        out[0, 1] = (-(rate * values[0, :, columns].astype(F32))).astype(BF16)


def prep(chain, keys, values, rates):
    info, token = chain
    groups, length, width = keys.shape
    heads = rates.shape[-1]
    part = width // heads
    return pl.pallas_call(
        prep_body,
        grid_spec=pltpu.PrefetchScalarGridSpec(
            num_scalar_prefetch=1,
            grid=(groups,),
            in_specs=[
                pl.BlockSpec((1, length, width), lambda i, info: (i, 0, 0)),
                pl.BlockSpec((1, length, width), lambda i, info: (i, 0, 0)),
                pl.BlockSpec((1, length, heads), lambda i, info: (i, 0, 0)),
                PASSED,
            ],
            out_specs=[pl.BlockSpec((1, 2, length, part), lambda i, info: (i, 0, 0, 0))] * heads
            + [PASSED],
        ),
        out_shape=[jax.ShapeDtypeStruct((groups, 2, length, part), BF16)] * heads
        + [TOKEN],
        input_output_aliases={4: heads},
        compiler_params=params(),
        cost_estimate=cost(0, 12 * groups * length * width),
        name="prep",
    )(info, keys, values, rates, token)


def tail_body(keys, values, token, *refs):
    for group, tail in enumerate(refs[:-1]):

        @pl.when(pl.program_id(0) == group)
        def _():
            tail[0] = keys[0]
            tail[1] = values[0]


def tail_copies(token, keys, values):
    groups, length, width = keys.shape
    block = pl.BlockSpec((1, length, width), lambda i: (i, 0, 0))
    return pl.pallas_call(
        tail_body,
        grid=(groups,),
        in_specs=[block] * 2 + [PASSED],
        out_specs=[pl.BlockSpec((2, length, width), lambda i: (0, 0, 0))] * groups + [PASSED],
        out_shape=[jax.ShapeDtypeStruct((2, length, width), keys.dtype)] * groups + [TOKEN],
        input_output_aliases={2: groups},
        compiler_params=params(),
        cost_estimate=cost(0, 8 * groups * length * width),
        name="tail_copies",
    )(keys, values, token)


def place_halves(info, target, own, other):
    rows = own.shape[0]
    target[pl.ds(pl.multiple_of(info[1] * rows, rows), rows), :] = own.astype(BF16)
    target[pl.ds(pl.multiple_of((1 - info[1]) * rows, rows), rows), :] = other.astype(BF16)


def grad_body(block, slots, info, *refs):
    parts = refs[:slots]
    own, other, token, out, token_out, weights, units, targets, hidden, gates, ups = refs[slots:]
    length = parts[0].shape[2]
    own, other = (ref if len(ref.shape) == 3 else ref.at[0] for ref in (own, other))
    for matrix in range(3):
        place_halves(info, weights.at[matrix], own[matrix], other[matrix])
    for slot, part in enumerate(parts):
        span = pl.ds(slot * length, length)
        key_unit = part[block, 0]
        target = part[block, 1]
        units[span, :] = key_unit
        targets[span, :] = target
        key_gate = dot(key_unit, weights[0])
        key_up = dot(key_unit, weights[1])
        back = dot_nt(target, weights[2])
        sig = sigmoid(key_gate)
        silu = key_gate * sig
        hidden[span, :] = (silu * key_up).astype(BF16)
        gates[span, :] = (back * key_up * sig * (1.0 + key_gate * (1.0 - sig))).astype(BF16)
        ups[span, :] = (back * silu).astype(BF16)
    rows = own.shape[1]
    for half in range(2):
        place = info[1] if half == 0 else 1 - info[1]
        columns = pl.ds(pl.multiple_of(place * rows, rows), rows)
        out[half, 0] = dot_tn(units[:, columns], gates[...]).astype(BF16)
        out[half, 1] = dot_tn(units[:, columns], ups[...]).astype(BF16)
        out[half, 2] = dot_tn(hidden[:, columns], targets[...]).astype(BF16)


def head_spec(shape):
    if len(shape) == 3:
        return pl.BlockSpec(memory_space=pltpu.VMEM)
    return pl.BlockSpec((1,) + shape[1:], lambda i, info: (info[0], 0, 0, 0))


def grad(block, chain, parts, own, other):
    info, token = chain
    slots = len(parts)
    _, _, length, width = parts[0].shape
    rows = own.shape[-2]
    total = slots * length
    return pl.pallas_call(
        functools.partial(grad_body, block, slots),
        grid_spec=pltpu.PrefetchScalarGridSpec(
            num_scalar_prefetch=1,
            grid=(1,),
            in_specs=[pl.BlockSpec(memory_space=pltpu.VMEM)] * slots
            + [head_spec(own.shape)] * 2
            + [PASSED],
            out_specs=[
                pl.BlockSpec((2, 3, rows, width), lambda i, info: (0, 0, 0, 0)),
                PASSED,
            ],
            scratch_shapes=[pltpu.VMEM((3, width, width), BF16)]
            + [pltpu.VMEM((total, width), BF16)] * 5,
        ),
        out_shape=[jax.ShapeDtypeStruct((2, 3, rows, width), BF16), TOKEN],
        input_output_aliases={3 + slots: 1},
        compiler_params=params(),
        cost_estimate=cost(12 * total * width * width, 4 * total * width + 15 * width * width),
        name="grad",
    )(info, *parts, own, other, token)


OWN_SKEW = 0
REST_SKEW = 0
CHUNK = 32


def fold(value):
    return jnp.sum(value.reshape(-1, 8, value.shape[-1]), axis=0)


def stages(rate, step, begun, gradient, moment, weight, put, x):
    rows = x.shape[0] // 2
    chunks = [(half, pl.ds(at, CHUNK)) for half in range(2) for at in range(0, rows, CHUNK)]
    held = {}

    def after(half, part):
        return rate * moment(half, part) + gradient(half, part)

    def stepped(half, part):
        return weight(half, part) - step * x[pl.ds(half * rows + part.start, CHUNK)].astype(F32)

    def begin():
        begun("moment")
        total = 0.0
        for half, part in chunks:
            value = after(half, part)
            total += fold(value * value)
        scale = lax.rsqrt(jnp.sum(total, keepdims=True) + 1e-06)
        for half, part in chunks:
            value = after(half, part)
            x[pl.ds(half * rows + part.start, CHUNK)] = (value * scale).astype(BF16)
            put("moment", half, part, value)
        put("moment", None, None, None)

    def gram():
        held["gram"] = dot_tn(x[...], x[...])

    def poly():
        half = held["gram"].astype(BF16)
        held["poly"] = (quintic_two * held["gram"] + quintic_three * dot(half, half)).astype(BF16)

    def turn():
        turned = quintic_one * x[...].astype(F32) + dot(x[...], held["poly"])
        x[...] = turned.astype(BF16)

    def finish():
        begun("weight")
        total = 0.0
        for half, part in chunks:
            value = stepped(half, part)
            total += fold(value * value)
        scale = lax.rsqrt(jnp.sum(total, axis=0, keepdims=True) + 1e-06)
        for half, part in chunks:
            put("weight", half, part, stepped(half, part) * scale)
        put("weight", None, None, None)

    return [begin] + [gram, poly, turn] * NS_STEPS + [finish]


def interleave(work, skew):
    for now in range(len(work[0]) + skew * (len(work) - 1)):
        for place, steps in enumerate(work):
            if 0 <= now - skew * place < len(steps):
                steps[now - skew * place]()


def own_body(info, rate, step, mine, theirs, *refs):
    state, (w_own, w_oth, token_out, moments, weights, x, load_sem) = refs[:4], refs[5:]
    head = info[0]
    matrices = w_own.shape[0]
    homes = [moments.at[0], moments.at[1], weights.at[0], weights.at[1]]
    loads = [
        [
            pltpu.make_async_copy(value.at[head, j], home.at[j], load_sem.at[i, j])
            for j in range(matrices)
        ]
        for i, (value, home) in enumerate(zip(state, homes))
    ]
    for group in loads:
        for load in group:
            load.start()

    def plan(j):
        def begun(kind):
            for i in (0, 1) if kind == "moment" else (2, 3):
                loads[i][j].wait()

        def put(kind, half, part, value):
            if kind == "weight" and half is not None:
                (w_own, w_oth)[half][j, part] = value.astype(BF16)

        return stages(
            rate[head], step[head], begun,
            lambda half, part: mine[half, j, part].astype(F32) + theirs[1 - half, j, part].astype(F32),
            lambda half, part: moments[half, j, part],
            lambda half, part: weights[half, j, part],
            put, x.at[j],
        )

    interleave([plan(j) for j in range(matrices)], OWN_SKEW)


def own_update(chain, rate, step, mine, theirs, state):
    info, token = chain
    _, matrices, rows, width = state[0].shape
    scalars = pl.BlockSpec(memory_space=pltpu.SMEM)
    near = pl.BlockSpec(memory_space=pltpu.VMEM)
    far = pl.BlockSpec(memory_space=pltpu.HBM)
    half = jax.ShapeDtypeStruct((matrices, rows, width), BF16)
    return pl.pallas_call(
        own_body,
        in_specs=[scalars] * 3 + [near] * 2 + [far] * 4 + [PASSED],
        out_specs=[near] * 2 + [PASSED],
        out_shape=[half, half, TOKEN],
        input_output_aliases={9: 2},
        scratch_shapes=[
            pltpu.VMEM((2, matrices, rows, width), F32),
            pltpu.VMEM((2, matrices, rows, width), F32),
            pltpu.VMEM((matrices, 2 * rows, width), BF16),
            pltpu.SemaphoreType.DMA((4, matrices)),
        ],
        compiler_params=params(),
        cost_estimate=cost(matrices * 6 * 2 * width**3, matrices * 16 * rows * width),
        name="own_update",
    )(info, rate, step, mine, theirs, *state, token)


def total_body(info, rate, first, first_other, second, second_other, token, own, oth, token_out):
    for half, out in enumerate((own, oth)):
        for matrix in range(out.shape[0]):
            for at in range(0, out.shape[1], CHUNK):
                part = pl.ds(at, CHUNK)
                early = first[half, matrix, part].astype(F32)
                early += first_other[1 - half, matrix, part].astype(F32)
                late = second[half, matrix, part].astype(F32)
                late += second_other[1 - half, matrix, part].astype(F32)
                out[matrix, part] = (rate[info[0]] * early + late).astype(BF16)


def total_gradient(chain, rate, pieces):
    info, token = chain
    _, matrices, rows, width = pieces[0].shape
    scalars = pl.BlockSpec(memory_space=pltpu.SMEM)
    near = pl.BlockSpec(memory_space=pltpu.VMEM)
    half = jax.ShapeDtypeStruct((matrices, rows, width), BF16)
    return pl.pallas_call(
        total_body,
        in_specs=[scalars] * 2 + [near] * 4 + [PASSED],
        out_specs=[near] * 2 + [PASSED],
        out_shape=[half, half, TOKEN],
        input_output_aliases={6: 2},
        compiler_params=params(),
        cost_estimate=cost(0, 20 * matrices * rows * width),
        name="total_gradient",
    )(info, rate, *pieces, token)


def last_body(slots, start, places, info, rate, step, *refs):
    ready, refs = refs[: 4 * slots], refs[4 * slots :]
    m_own, m_oth = refs[:2]
    m_out, w_out, token_out, held, x = refs[-5:]
    head = info[0] ^ (pl.program_id(0) + start)
    for slot in range(slots):

        @pl.when(pl.program_id(0) == slot)
        def _():
            for i in range(4):
                held[i] = pick(ready[4 * slot + i], places[4 * slot + i])[...]

    def plan(j):
        def put(kind, half, part, value):
            if half == 0:
                (m_out if kind == "moment" else w_out)[0, j, part] = value

        return stages(
            rate[head] * rate[head], step[head], lambda kind: None,
            lambda half, part: held[half, j, part].astype(F32),
            lambda half, part: (m_own, m_oth)[half][0, j, part],
            lambda half, part: held[2 + half, j, part].astype(F32),
            put, x.at[j],
        )

    interleave([plan(j) for j in range(m_own.shape[1])], REST_SKEW)


def last_update(chain, rate, step, gradients, weights, state, previous, start):
    info, token = chain
    heads, matrices, rows, width = state[0].shape
    slots = len(gradients)
    block = pl.BlockSpec((1, matrices, rows, width), lambda s, info: (info[0] ^ (s + start), 0, 0, 0))
    scalars = pl.BlockSpec(memory_space=pltpu.SMEM)
    near = pl.BlockSpec(memory_space=pltpu.VMEM)
    far = pl.BlockSpec(memory_space=pltpu.HBM)
    full = jax.ShapeDtypeStruct((heads, matrices, rows, width), F32)
    kept = list(previous or [])
    ready = [value for pair in zip(gradients, weights) for both in pair for value in both]
    places = [at for _, at in ready]
    ready = [value for value, _ in ready]
    return pl.pallas_call(
        functools.partial(last_body, slots, start, places),
        grid_spec=pltpu.PrefetchScalarGridSpec(
            num_scalar_prefetch=1,
            grid=(slots,),
            in_specs=[scalars] * 2 + [near] * (4 * slots) + [block] * 2 + [far] * len(kept)
            + [PASSED],
            out_specs=[block] * 2 + [PASSED],
            scratch_shapes=[
                pltpu.VMEM((4, matrices, rows, width), BF16),
                pltpu.VMEM((matrices, 2 * rows, width), BF16),
            ],
        ),
        out_shape=[full] * 2 + [TOKEN],
        input_output_aliases={5 + 4 * slots + i: i for i in range(len(kept))}
        | {5 + 4 * slots + len(kept): 2},
        compiler_params=params(),
        cost_estimate=cost(
            slots * matrices * 6 * 2 * width**3, slots * matrices * 16 * rows * width
        ),
        name="last_update",
    )(info, rate, step, *ready, *state, *kept, token)


def gate_body(*refs):
    pass


def gate(token, values):
    count = len(values) + 1
    return pl.pallas_call(
        gate_body,
        in_specs=[PASSED] * count,
        out_specs=[PASSED] * count,
        out_shape=[jax.ShapeDtypeStruct(value.shape, value.dtype) for value in values] + [TOKEN],
        input_output_aliases={i: i for i in range(count)},
        compiler_params=params(),
        cost_estimate=cost(0, 0),
        name="gate",
    )(*values, token)


def relay_body(x, y, token, both, to_x, to_y, token_out):
    rows = to_x.shape[1]
    both[0] = x[...]
    both[1] = y[...]
    to_x[...] = y[:, :rows]
    to_y[...] = x[:, rows:]


def relay(token, x, y):
    matrices, rows, width = x.shape
    near = pl.BlockSpec(memory_space=pltpu.VMEM)
    part = jax.ShapeDtypeStruct((matrices, rows // 2, width), x.dtype)
    return pl.pallas_call(
        relay_body,
        in_specs=[near] * 2 + [PASSED],
        out_specs=[near] * 3 + [PASSED],
        out_shape=[jax.ShapeDtypeStruct((2,) + x.shape, x.dtype), part, part, TOKEN],
        input_output_aliases={2: 3},
        compiler_params=params(),
        cost_estimate=cost(0, 6 * x.size),
        name="relay",
    )(x, y, token)


def join_body(from_x, from_y, token, out, token_out):
    rows = from_x.shape[1]
    out[:, :rows] = from_x[...]
    out[:, rows:] = from_y[...]


def join(token, from_x, from_y):
    matrices, rows, width = from_x.shape
    near = pl.BlockSpec(memory_space=pltpu.VMEM)
    return pl.pallas_call(
        join_body,
        in_specs=[near] * 2 + [PASSED],
        out_specs=[near, PASSED],
        out_shape=[jax.ShapeDtypeStruct((matrices, 2 * rows, width), from_x.dtype), TOKEN],
        input_output_aliases={2: 1},
        compiler_params=params(),
        cost_estimate=cost(0, 8 * from_x.size),
        name="join",
    )(from_x, from_y, token)


def pick(ref, at):
    return ref if at is None else ref.at[at]


def place_all(info, weights, halves, step):
    if len(halves[0][0].shape) == 4 and halves[0][1] is None:
        for matrix in range(weights.shape[0]):
            own, other = (ref[0, matrix] for ref, _ in halves)
            place_halves(info, weights.at[matrix], own, other)
        return
    for slot in range(len(halves) // 2):

        @pl.when(step == slot)
        def _():
            own, other = (pick(ref, at) for ref, at in halves[2 * slot : 2 * slot + 2])
            for matrix in range(weights.shape[0]):
                place_halves(info, weights.at[matrix], own[matrix], other[matrix])


def recall(query_unit, weights):
    gate = dot(query_unit, weights[0])
    hidden = (gate * sigmoid(gate) * dot(query_unit, weights[1])).astype(BF16)
    return dot(hidden, weights[2])


def attend(block, info, query, key, value, early_keys, early_values):
    length, width = query.shape
    rows = lax.broadcasted_iota(jnp.int32, (length, length), 0)
    lanes = lax.broadcasted_iota(jnp.int32, (length, length), 1)
    here = lanes <= rows
    early_key, early_value = early_keys[0], early_values[0]
    if block:
        early_key = jnp.where(info[2] == 1, early_key, early_keys[1])
        early_value = jnp.where(info[2] == 1, early_value, early_values[1])
    scores = dot_nt(query, early_key)
    if block == 0:
        scores = scores + jnp.where(info[2] == 1, -1e30, 0.0)
    scores = jnp.where(here, dot_nt(query, key), scores)
    top = jnp.max(scores, axis=1, keepdims=True)
    expo = jnp.exp2((scores - top) * (width ** (-0.5) * float(np.log2(np.e))))
    total = jnp.sum(expo, axis=1, keepdims=True)
    result = dot(jnp.where(here, expo, 0.0).astype(BF16), value)
    result += dot(jnp.where(here, 0.0, expo).astype(BF16), early_value)
    return result * (1.0 / total)


def mix_body(block, attends, places, info, queries, *refs):
    held = len(places)
    if attends:
        keys, values, *refs = refs
        early, refs = refs[: 2 + 2 * block], refs[2 + 2 * block :]
    else:
        attended, *refs = refs
    halves, refs = refs[:held], refs[held:]
    kept = len(refs) - 2 - (held > 0)
    out, token_out, *weights = refs[kept:]
    recalled = None
    if held:
        place_all(info, weights[0], list(zip(halves, places)), pl.program_id(0))
        recalled = recall(unit(queries[0]), weights[0])
    if not attends:
        out[0] = (attended[0] + recalled).astype(out.dtype)
        return
    for head in range(queries.shape[2] // HEAD_DIM):
        columns = slice(head * HEAD_DIM, (head + 1) * HEAD_DIM)
        result = attend(
            block, info, queries[0, :, columns], keys[0, :, columns], values[0, :, columns],
            [value[0, :, columns] for value in early[::2]],
            [value[0, :, columns] for value in early[1::2]],
        )
        if held:
            result = result + recalled[:, columns]
        out[0, :, columns] = result.astype(out.dtype)


def mix(block, chain, queries, heads, attention, halves, attended=None, previous=None, slots=None):
    info, token = chain
    groups, length, width = queries.shape
    part = width // heads
    start, stop = slots or (0, heads)

    def columns(at):
        return pl.BlockSpec((1, length, part), lambda s, info: (at, 0, info[0] ^ (s + start)))

    values, specs = [queries], [columns(block)]
    if attention:
        keys_values, early = attention
        values += keys_values + [value for value, _ in early]
        specs += [columns(block)] * 2 + [columns(at) for _, at in early]
    else:
        values.append(attended)
        specs.append(columns(0))
    places = [at for _, at in halves]
    halves = [value for value, _ in halves]
    values += halves
    if halves and halves[0].ndim == 4 and places[0] is None:
        shape = (1,) + halves[0].shape[1:]
        specs += [pl.BlockSpec(shape, lambda s, info: (info[0] ^ s, 0, 0, 0))] * 2
    else:
        specs += [pl.BlockSpec(memory_space=pltpu.VMEM)] * len(halves)
    aliases = {}
    if previous is not None:
        aliases = {1 + len(values): 0}
        values.append(previous)
        specs.append(pl.BlockSpec(memory_space=pltpu.HBM))
    aliases[1 + len(values)] = 1
    values.append(token)
    specs.append(PASSED)
    if halves:
        out, place = jax.ShapeDtypeStruct(queries.shape, BF16), block
    else:
        out, place = jax.ShapeDtypeStruct((1, length, width), F32), 0
    return pl.pallas_call(
        functools.partial(mix_body, block, attention is not None, places),
        grid_spec=pltpu.PrefetchScalarGridSpec(
            num_scalar_prefetch=1,
            grid=(stop - start,),
            in_specs=specs,
            out_specs=[columns(place), PASSED],
            scratch_shapes=[pltpu.VMEM((3, part, part), BF16)] if halves else [],
        ),
        out_shape=[out, TOKEN],
        input_output_aliases=aliases,
        compiler_params=params(),
        cost_estimate=cost((attention is not None) * 4e11, 0),
        name="mix",
    )(info, *values)


def owner_shards(queries, keys, values, token_lr, momentum_rate, update_step, fast_weights, momentum):
    groups, length, _ = queries.shape
    chips = lax.axis_size("tok")
    chip = lax.axis_index("tok")
    row = lax.axis_index("row")
    first = (lax.axis_index(("tok", "row")) == 0).astype(jnp.int32)
    info = jnp.stack([chip, row, first]).astype(jnp.int32)
    rates = jnp.transpose(token_lr, (1, 2, 0))
    scalars = (momentum_rate, update_step)

    def to_chip(value, slot):
        return lax.ppermute(value, "tok", [(c, c ^ slot) for c in range(chips)])

    def to_core(value):
        return lax.ppermute(value, "row", [(0, 1), (1, 0)])

    def pass_on(piece, wrap):
        places = chips * lax.axis_size("row")
        pairs = [(d, (d + 1) % places) for d in range(places - (not wrap))]
        return lax.ppermute(piece, ("tok", "row"), pairs)

    state = (momentum, to_core(momentum), fast_weights, to_core(fast_weights))
    token = jnp.zeros(TOKEN.shape, TOKEN.dtype)
    *sent, token = prep((info, token), keys, values, rates)
    parts = [sent[0]] + [to_chip(sent[slot], slot) for slot in range(1, chips)]
    tail, last_tail, token = tail_copies(token, keys, values)
    first, token = grad(0, (info, token), parts, *state[2:])
    tail, token = gate(token, [tail])
    tail = pass_on(tail, True)
    pair = [keys, values]
    early = [(tail, at) for at in range(2)]
    pieces = [first, to_core(first)]
    w_own, w_oth, token = own_update((info, token), *scalars, *pieces, state)
    w_x, w_y = (to_chip(w_own, slot) for slot in (1, 2))
    second, token = grad(1, (info, token), parts, w_own, w_oth)
    pieces += [second, to_core(second)]
    g_own, g_oth, token = total_gradient((info, token), momentum_rate, pieces)
    g_x, g_y = (to_chip(g_own, slot) for slot in (1, 2))
    halves = [(value, None) for value in state[2:]]
    mixed, token = mix(0, (info, token), queries, chips, (pair, early), halves)

    def both_halves(value):
        return value, to_core(value)

    def each(halves, at=None):
        return [(half, at) for half in halves]

    def across(token, x, y):
        near, to_x, to_y, token = relay(token, x, y)
        near = both_halves(near)
        return [each(near, 0), each(near, 1)], (to_chip(to_x, 1), to_chip(to_y, 2)), token

    def last(token, gradients, weights, done, start):
        return last_update((info, token), *scalars, gradients, weights, state[:2], done, start)

    w_all = [each(both_halves(w_own))]
    *done, token = last(token, [each((g_own, g_oth))], w_all, None, 0)
    w_near, w_far, token = across(token, w_x, w_y)
    last_tail, token = gate(token, [last_tail])
    last_tail = pass_on(last_tail, False)
    early += [(last_tail, at) for at in range(2)]
    g_near, g_far, token = across(token, g_x, g_y)
    *done, token = last(token, g_near, w_near, done, 1)
    attended, token = mix(1, (info, token), queries, chips, (pair, early), [])
    w_far, token = join(token, *w_far)
    w_far = each(both_halves(w_far))
    halves = [value for both in w_all + w_near + [w_far] for value in both]
    mixed, token = mix(1, (info, token), queries, chips, None, halves, attended, mixed)
    g_far, token = join(token, *g_far)
    g_far = each(both_halves(g_far))
    moment, weights, token = last(token, [g_far], [w_far], done, 3)
    return (mixed, weights, moment)


def shards(chips, queries, *rest):
    heads = queries.shape[2] // DH
    if heads == chips == 4 and queries.shape[:2] == (GROUPS, WINDOW):
        return owner_shards(queries, *rest)
    return general_shards(queries, *rest)


def solution(mesh):
    return jax.shard_map(
        functools.partial(shards, mesh.shape["tok"]),
        mesh=mesh,
        in_specs=(
            P(None, ("tok", "row"), "mem"),
            P(None, ("tok", "row"), "mem"),
            P(None, ("tok", "row"), "mem"),
            P("mem", None, ("tok", "row")),
            P("mem"),
            P("mem"),
            P("mem", None, "row", None),
            P("mem", None, "row", None),
        ),
        out_specs=(
            P(None, ("tok", "row"), "mem"),
            P("mem", None, "row", None),
            P("mem", None, "row", None),
        ),
        check_vma=False,
    )
```
